128 devices in a mesh: space: 32 (over y, z_lo, x), group: 4 (over z_hi, core).
Axes of the slice: x: 4, y: 4, z: 4 (z_hi: 2, z_lo: 2; z = z_hi * 2 + z_lo), core: 2. Of those that a mesh axis runs over, the one named last changes fastest.
Arguments:
- source: float32 [512, 256, 256], P('space', 'group'), may hold values from -4.5 to 6.5
- phases: int32 [512, 256, 256], P('space', 'group'), may hold values from 0 to 7
Outputs:
- pressure: float32 [512, 256, 256], P('space', 'group')
- residual: float32 [512, 256, 256], P('space', 'group')
The draws below stay inside these ranges and needn't reach their ends.
All inputs are finite; a program needn't handle non-finite values.
Results may differ from the reference program's by a relative error of at most 0.0003.
Values sent between devices are 32-bit elements; how exact they have to be, the bound alone decides.
A program may use at most 192 MiB of HBM per device.

```python
import math
import jax
import jax.numpy as jnp

PRE = 2
POST = 2
CHEB = 6
PHASES = 8
NX = 512
NY = 256
NZ = 256


def draw_source(key, part):
    position = jnp.arange(NX, dtype=jnp.float32)[:, None, None] / NX
    noise = jnp.clip(jax.random.normal(key, (NX, NY, NZ), jnp.float32), -5.0, 5.0)
    return noise + (0.5 + position)


def plant(entries, stream_key, smallest, top_value):
    index_at = [jax.random.randint(jax.random.fold_in(stream_key, axis), (), 0, length) for axis, length in enumerate(entries.shape)]
    main_axis = entries.shape.index(max(entries.shape))
    beside = index_at[:main_axis] + [(index_at[main_axis] + 1) % entries.shape[main_axis]] + index_at[main_axis + 1:]
    return entries.at[tuple(index_at)].set(smallest).at[tuple(beside)].set(top_value)


def setup_inputs(seed: int = 0) -> dict:
    streams_of = jax.random.split(jax.random.key(seed), 3)
    return {
        "source": draw_source(jax.random.fold_in(streams_of[2], 71), 0),
        "phases": plant(jax.random.randint(streams_of[1], (NX, NY, NZ), 0, PHASES), jax.random.fold_in(streams_of[1], 1), 0, PHASES - 1).astype(jnp.int32),
    }


REACTION = 0.01
RELAX = 0.8
LOWER = 0.05
UPPER = 2.0


def conductivity(phases):
    return jnp.exp(phases.astype(jnp.float32) * (-6.0 * math.log(10.0) / (PHASES - 1)))


def harmonic(left, right):
    return 2.0 * left * right / (left + right)


def face_weights(kpadded):
    center = kpadded[1:-1, 1:-1, 1:-1]
    return (harmonic(center, kpadded[2:, 1:-1, 1:-1]), harmonic(center, kpadded[:-2, 1:-1, 1:-1]),
            harmonic(center, kpadded[1:-1, 2:, 1:-1]), harmonic(center, kpadded[1:-1, :-2, 1:-1]),
            harmonic(center, kpadded[1:-1, 1:-1, 2:]), harmonic(center, kpadded[1:-1, 1:-1, :-2]))


def stencil(center, padded, weights):
    field = padded[1:-1, 1:-1, 1:-1]
    beside_all = weights[0] * padded[2:, 1:-1, 1:-1] + weights[1] * padded[:-2, 1:-1, 1:-1]
    beside_all = beside_all + weights[2] * padded[1:-1, 2:, 1:-1] + weights[3] * padded[1:-1, :-2, 1:-1]
    beside_all = beside_all + weights[4] * padded[1:-1, 1:-1, 2:] + weights[5] * padded[1:-1, 1:-1, :-2]
    return center * field - beside_all


def collapse_x(array):
    extent = array.shape
    return array.reshape(extent[0], extent[1] // 2, 2, extent[2] // 2, 2).sum(axis=(2, 4))


def collapse_y(array):
    extent = array.shape
    return array.reshape(extent[0] // 2, 2, extent[1], extent[2] // 2, 2).sum(axis=(1, 4))


def collapse_z(array):
    extent = array.shape
    return array.reshape(extent[0] // 2, 2, extent[1] // 2, 2, extent[2]).sum(axis=(1, 3))


def collapse_all(array):
    extent = array.shape
    return array.reshape(extent[0] // 2, 2, extent[1] // 2, 2, extent[2] // 2, 2).sum(axis=(1, 3, 5))


def coarse_operator(kappa, weights):
    east = collapse_x(weights[0][1::2])
    west = collapse_x(weights[1][0::2])
    north = collapse_y(weights[2][:, 1::2])
    south = collapse_y(weights[3][:, 0::2])
    upper = collapse_z(weights[4][:, :, 1::2])
    lower = collapse_z(weights[5][:, :, 0::2])
    center = collapse_all(REACTION * kappa) + east + west + north + south + upper + lower
    return (east, west, north, south, upper, lower, center)


def expand_blocks(coarse):
    extent = coarse.shape
    spread = jnp.broadcast_to(coarse[:, None, :, None, :, None], (extent[0], 2, extent[1], 2, extent[2], 2))
    return spread.reshape(2 * extent[0], 2 * extent[1], 2 * extent[2])


def chebyshev(forcing, coefs, padder):
    weights = coefs[:6]
    center = coefs[6]
    theta = (UPPER + LOWER) / 2.0
    delta = (UPPER - LOWER) / 2.0
    ratio = delta / theta
    correction = jnp.zeros_like(forcing)
    remainder = forcing
    heading = (remainder / center) * (1.0 / theta)
    for turn in range(CHEB):
        correction = correction + heading
        if turn + 1 < CHEB:
            remainder = remainder - stencil(center, padder(heading), weights)
            following = 1.0 / (2.0 * theta / delta - ratio)
            heading = (following * ratio) * heading + (2.0 * following / delta) * (remainder / center)
            ratio = following
    return correction


def reference(source, phases):
    kappa = conductivity(phases)
    weights = face_weights(jnp.pad(kappa, 1))
    diagonal = REACTION * kappa + weights[0] + weights[1] + weights[2] + weights[3] + weights[4] + weights[5]
    average = jnp.sum(source) / source.size
    forcing = kappa * (source - average)

    def residual_of(current):
        return forcing - stencil(diagonal, jnp.pad(current, 1), weights)

    def relax(current, remainder):
        return current + RELAX * (remainder / diagonal)

    pressure = jnp.zeros(source.shape, jnp.float32)
    residual = forcing
    for sweep in range(PRE):
        pressure = relax(pressure, residual)
        residual = residual_of(pressure)
    coarse_forcing = collapse_all(residual)
    coefs = coarse_operator(kappa, weights)
    correction = chebyshev(coarse_forcing, coefs, lambda field: jnp.pad(field, 1))
    pressure = pressure + expand_blocks(correction)
    residual = residual_of(pressure)
    for sweep in range(POST):
        pressure = relax(pressure, residual)
        residual = residual_of(pressure)
    return pressure, residual
```

```python
import functools
import math

import jax
import jax.numpy as jnp
from jax import lax
from jax.experimental import pallas as pl
from jax.experimental.pallas import tpu as pltpu
from jax.sharding import PartitionSpec as P

CHEB = 6
PHASES = 8
REACTION = 0.01
RELAX = 0.8
LOWER = 0.05
UPPER = 2.0

F32 = jnp.float32
MESH = pl.DeviceIdType.MESH

PX, PY, LANES = 16, 64, 128
X0, Y0 = 4, 8
FX, FY = PX + 2 * X0, PY + 2 * Y0
W = 3
R0, RN = 4, 72
CX, CY = PX // 2, PY // 2
CW, CX0, CY0 = 7, 7, 8
GX, GY = CX + 2 * CX0, CY + 2 * CY0
DIRS = [(-1, 0), (1, 0), (0, -1), (0, 1), (-1, -1), (-1, 1), (1, -1), (1, 1)]
NO_CELL = 1 << 20


def spans(step, start, size, width):
    if step == 0:
        return pl.ds(start, size), pl.ds(start, size)
    if step > 0:
        return pl.ds(start + size - width, width), pl.ds(start - width, width)
    return pl.ds(start, width), pl.ds(start + size, width)


def fine_spans(dx, dy, wx, wy):
    return spans(dx, X0, PX, wx), spans(dy, Y0, PY, wy)


def coarse_spans(dx, dy):
    return spans(dx, CX0, CX, CW), spans(dy, CY0, CY, CY0)


def harmonic(left, right):
    return 2.0 * left * right / jnp.maximum(left + right, 1e-30)


def pieces(x):
    high = x.astype(jnp.bfloat16)
    rest = x - high.astype(F32)
    mid = rest.astype(jnp.bfloat16)
    low = (rest - mid.astype(F32)).astype(jnp.bfloat16)
    return high, mid, low


def zdot(x, matrix):
    high, mid, low = pieces(x)
    dot = functools.partial(jnp.dot, preferred_element_type=F32)
    return dot(high, matrix) + dot(mid, matrix) + dot(low, matrix)


def kernel(
    ns, ng, source_hbm, phases_hbm, out_p, out_r,
    ph, src, kap, wx, wy, wz, dg, di, fo, pa, pb, pc, res,
    cw, rem, cinv, ha, hb, cor, zbuf, ybuf, ebuf,
    part, sum1, sum2,
    in_sem, out_sem, psend, precv, send, recv,
):
    s, g = lax.axis_index("space"), lax.axis_index("group")
    lane = lax.broadcasted_iota(jnp.int32, (1, LANES), 1)

    def here(dx, dy):
        ok = jnp.bool_(True)
        if dx < 0:
            ok = s > 0
        if dx > 0:
            ok = s < ns - 1
        if dy < 0:
            ok = jnp.logical_and(ok, g > 0)
        if dy > 0:
            ok = jnp.logical_and(ok, g < ng - 1)
        return ok

    def halves(hbm, ref, sem):
        return [
            pltpu.make_async_copy(
                hbm.at[:, :, pl.ds(h * LANES, LANES)],
                ref.at[h, pl.ds(X0, PX), pl.ds(Y0, PY)],
                sem.at[h],
            )
            for h in range(2)
        ]

    load_ph = halves(phases_hbm, ph, in_sem.at[0])
    load_src = halves(source_hbm, src, in_sem.at[1])
    for copy in load_ph + load_src:
        copy.start()

    x4, q = lax.rem(s, 4), s // 4
    nq = ns // 4
    n1 = 4 * ng
    me1 = x4 * ng + g

    def peer1(j):
        t = lax.rem(me1 + j, n1)
        return (q * 4 + t // ng, lax.rem(t, ng))

    def peer2(j):
        return (lax.rem(q + j, nq) * 4 + x4, g)

    barrier = pltpu.get_barrier_semaphore()
    expected = jnp.int32(n1 - 1 + nq - 1)

    def greet(peer):
        pl.semaphore_signal(barrier, inc=1, device_id=peer, device_id_type=MESH)

    for dx, dy in DIRS:
        ok = here(dx, dy)

        @pl.when(ok)
        def _():
            greet((s + dx, g + dy))

        expected = expected + ok.astype(jnp.int32)
    for j in range(1, n1):
        greet(peer1(j))
    for j in range(1, nq):
        greet(peer2(j))

    for dx, dy in DIRS:

        @pl.when(jnp.logical_not(here(-dx, -dy)))
        def _():
            (_, tx), (_, ty) = fine_spans(dx, dy, W, Y0)
            (_, ux), (_, uy) = coarse_spans(dx, dy)
            shape = ph[:, tx, ty].shape
            ph[:, tx, ty] = jnp.full(shape, NO_CELL, jnp.int32)
            src[:, tx, ty] = jnp.zeros(shape, F32)
            pc[:, tx, ty] = jnp.zeros(shape, F32)
            cw[:, ux, uy] = jnp.zeros(cw[:, ux, uy].shape, F32)
            rem[ux, uy] = jnp.zeros(rem[ux, uy].shape, F32)

    def exchange(stage, src_at, dst_at):
        def copy(k, dx, dy):
            return pltpu.make_async_remote_copy(
                src_ref=src_at(dx, dy),
                dst_ref=dst_at(dx, dy),
                send_sem=send.at[stage, k],
                recv_sem=recv.at[stage, k],
                device_id=(s + dx, g + dy),
                device_id_type=MESH,
            )

        def start():
            for k, (dx, dy) in enumerate(DIRS):

                @pl.when(here(dx, dy))
                def _():
                    copy(k, dx, dy).start()

        def wait_recv():
            for k, (dx, dy) in enumerate(DIRS):

                @pl.when(here(-dx, -dy))
                def _():
                    copy(k, dx, dy).wait_recv()

        def wait_send():
            for k, (dx, dy) in enumerate(DIRS):

                @pl.when(here(dx, dy))
                def _():
                    copy(k, dx, dy).wait_send()

        return start, wait_recv, wait_send

    def fine_exchange(stage, a, b, width):
        def src_at(dx, dy):
            (sx, _), (sy, _) = fine_spans(dx, dy, width, width)
            return a.at[:, sx, sy]

        def dst_at(dx, dy):
            (_, tx), (_, ty) = fine_spans(dx, dy, width, width)
            return b.at[:, tx, ty]

        return exchange(stage, src_at, dst_at)

    def coarse_exchange(stage, a, lead):
        def src_at(dx, dy):
            (sx, _), (sy, _) = coarse_spans(dx, dy)
            return a.at[:, sx, sy] if lead else a.at[sx, sy]

        def dst_at(dx, dy):
            (_, tx), (_, ty) = coarse_spans(dx, dy)
            return a.at[:, tx, ty] if lead else a.at[tx, ty]

        return exchange(stage, src_at, dst_at)

    ph_start, ph_recv, ph_sent = fine_exchange(0, ph, ph, W)
    src_start, src_recv, src_sent = fine_exchange(1, src, src, W - 1)
    cw_start, cw_recv, cw_sent = coarse_exchange(2, cw, True)
    rem_start, rem_recv, rem_sent = coarse_exchange(3, rem, False)
    p_start, p_recv, p_sent = fine_exchange(4, pb, pc, W)

    for copy in load_src:
        copy.wait()

    def add_plane(x, total):
        plane = src[0, x, pl.ds(Y0, PY)] + src[1, x, pl.ds(Y0, PY)]
        return total + jnp.sum(plane.reshape(PY // 8, 8, LANES), axis=0)

    local = lax.fori_loop(X0, X0 + PX, add_plane, jnp.zeros((8, LANES), F32))
    local = jnp.sum(local, axis=0, keepdims=True)
    part[0] = local
    sum1[me1] = local
    for copy in load_ph:
        copy.wait()

    pl.semaphore_wait(barrier, expected)

    def gather_part(stage, slots, count, me, peer):
        def start():
            for j in range(1, count):
                pltpu.make_async_remote_copy(
                    src_ref=part.at[stage],
                    dst_ref=slots.at[me],
                    send_sem=psend.at[stage],
                    recv_sem=precv.at[stage],
                    device_id=peer(j),
                    device_id_type=MESH,
                ).start()

        def wait():
            pltpu.make_async_remote_copy(
                src_ref=slots.at[pl.ds(0, count - 1)],
                dst_ref=slots.at[pl.ds(0, count - 1)],
                send_sem=psend.at[stage],
                recv_sem=precv.at[stage],
                device_id=peer(1),
                device_id_type=MESH,
            ).wait()

        return start, wait

    start1, wait1 = gather_part(0, sum1, n1, me1, peer1)
    start2, wait2 = gather_part(1, sum2, nq, q, peer2)
    start1()
    ph_start()
    src_start()

    def conductivity(x, r0, n):
        for h in range(2):
            kap[h, x, pl.ds(r0, n)] = jnp.exp(
                ph[h, x, pl.ds(r0, n)].astype(F32) * (-6.0 * math.log(10.0) / (PHASES - 1))
            )

    def faces(x, r0, n):
        rows, above = pl.ds(r0, n), pl.ds(r0 + 1, n)
        k = [kap[h, x, rows] for h in range(2)]
        up = [pltpu.roll(k[h], LANES - 1, 1) for h in range(2)]
        last = lane == LANES - 1
        beside = [jnp.where(last, up[1], up[0]), jnp.where(last, 0.0, up[1])]
        for h in range(2):
            wx[h, x, rows] = harmonic(k[h], kap[h, x + 1, rows])
            wy[h, x, rows] = harmonic(k[h], kap[h, x, above])
            wz[h, x, rows] = harmonic(k[h], beside[h])

    def diagonal(x, r0, n):
        rows, below = pl.ds(r0, n), pl.ds(r0 - 1, n)
        z = [wz[h, x, rows] for h in range(2)]
        down = [pltpu.roll(z[h], 1, 1) for h in range(2)]
        first = lane == 0
        beside = [jnp.where(first, 0.0, down[0]), jnp.where(first, down[0], down[1])]
        for h in range(2):
            d = REACTION * kap[h, x, rows] + wx[h, x, rows] + wx[h, x - 1, rows]
            d = d + wy[h, x, rows] + wy[h, x, below] + z[h] + beside[h]
            dg[h, x, rows] = d
            di[h, x, rows] = jnp.where(d > 0.0, RELAX / jnp.where(d > 0.0, d, 1.0), 0.0)

    def planes(lo, hi, body):
        def step(x, carry):
            body(x)
            return carry

        lax.fori_loop(lo, hi, step, 0)

    planes(X0, X0 + PX, lambda x: conductivity(x, Y0, PY))

    def inner(x):
        faces(x, Y0, PY)

    planes(X0, X0 + PX - 1, inner)

    wait1()
    total1 = jnp.sum(sum1[...], axis=0)
    part[1] = total1
    sum2[q] = total1
    start2()

    planes(X0 + 1, X0 + PX - 1, lambda x: diagonal(x, Y0, PY))

    ph_recv()

    def halo_conductivity(x):
        conductivity(x, 0, 8)
        conductivity(x, FY - 8, 8)

    planes(X0, X0 + PX, halo_conductivity)
    for lo in (X0 - W, X0 + PX):
        planes(lo, lo + W, lambda x: conductivity(x, 0, FY))
    for lo, hi in ((X0 - W, X0 + 1), (X0 + PX - 1, X0 + PX + W - 1)):
        planes(lo, hi, lambda x: faces(x, R0, RN))

    def edge_faces(x):
        faces(x, R0, 8)
        faces(x, R0 + RN - 8, 8)

    planes(X0 + 1, X0 + PX - 1, edge_faces)
    for lo, hi in ((X0 - W + 1, X0 + 1), (X0 + PX - 1, X0 + PX + W - 1)):
        planes(lo, hi, lambda x: diagonal(x, R0, RN))

    def edge_diagonal(x):
        diagonal(x, R0, 8)
        diagonal(x, R0 + RN - 8, 8)

    planes(X0 + 1, X0 + PX - 1, edge_diagonal)

    z_in = lax.broadcasted_iota(jnp.int32, (2 * LANES, LANES), 0)
    z_out = lax.broadcasted_iota(jnp.int32, (2 * LANES, LANES), 1)
    both = jnp.where(z_in // 2 == z_out, 1.0, 0.0).astype(jnp.bfloat16)
    upper = jnp.where(z_in == 2 * z_out + 1, 1.0, 0.0).astype(jnp.bfloat16)
    outer = jnp.where(z_in == 2 * z_out + 1, 1.0, 0.0) + jnp.where(z_in == 2 * z_out - 1, 1.0, 0.0)
    outer = outer.astype(jnp.bfloat16)

    even, odd = pl.ds(Y0, CY, stride=2), pl.ds(Y0 + 1, CY, stride=2)
    under = pl.ds(Y0 - 1, CY, stride=2)

    def coarse_parts(i, carry):
        a = X0 + 2 * i
        b = a + 1
        rows = pl.ds(pl.multiple_of(i * CY, CY), CY)
        for h in range(2):
            cols = pl.ds(h * LANES, LANES)

            def pair(ref, x):
                return ref[h, x, even] + ref[h, x, odd]

            east = pair(wx, b)
            north = wy[h, a, odd] + wy[h, b, odd]
            south = wy[h, a, under] + wy[h, b, under]
            kept = REACTION * (pair(kap, a) + pair(kap, b))
            zbuf[0, rows, cols] = east
            zbuf[1, rows, cols] = north
            zbuf[2, rows, cols] = pair(wz, a) + pair(wz, b)
            zbuf[3, rows, cols] = kept + east + pair(wx, a - 1) + north + south
        return carry

    lax.fori_loop(0, CX, coarse_parts, 0)

    own = (pl.ds(CX0, CX), pl.ds(CY0, CY))
    cube = (CX, CY, LANES)
    cw[(0,) + own] = zdot(zbuf[0], both).reshape(cube)
    cw[(1,) + own] = zdot(zbuf[1], both).reshape(cube)
    cw[(2,) + own] = zdot(zbuf[2], upper).reshape(cube)
    cw[(3,) + own] = (zdot(zbuf[3], both) + zdot(zbuf[2], outer)).reshape(cube)
    cw_start()

    wait2()
    total = jnp.sum(sum2[...], axis=0)
    average = jnp.sum(total, axis=1, keepdims=True) * (1.0 / (PX * ns * PY * ng * 2 * LANES))
    src_recv()

    rows = pl.ds(R0, RN)

    def first_sweep(x):
        for h in range(2):
            f = kap[h, x, rows] * (src[h, x, rows] - average)
            fo[h, x, rows] = f
            pa[h, x, rows] = di[h, x, rows] * f

    planes(X0 - W + 1, X0 + PX + W - 1, first_sweep)

    def beside_sum(p, x, r0, n):
        mid, above, below = pl.ds(r0, n), pl.ds(r0 + 1, n), pl.ds(r0 - 1, n)
        v = [p[h, x, mid] for h in range(2)]
        z = [wz[h, x, mid] for h in range(2)]
        up = [pltpu.roll(v[h], LANES - 1, 1) for h in range(2)]
        down = [pltpu.roll(z[h] * v[h], 1, 1) for h in range(2)]
        up[0] = jnp.where(lane == LANES - 1, up[1], up[0])
        first = lane == 0
        down = [jnp.where(first, 0.0, down[0]), jnp.where(first, down[0], down[1])]
        sums = []
        for h in range(2):
            t = wx[h, x, mid] * p[h, x + 1, mid] + wx[h, x - 1, mid] * p[h, x - 1, mid]
            t = t + wy[h, x, mid] * p[h, x, above] + wy[h, x, below] * p[h, x, below]
            sums.append(t + z[h] * up[h] + down[h])
        return v, sums

    def sweep(old, new):
        def body(x):
            v, t = beside_sum(old, x, R0, RN)
            for h in range(2):
                new[h, x, rows] = (1.0 - RELAX) * v[h] + di[h, x, rows] * (fo[h, x, rows] + t[h])

        return body

    def residual(p, x):
        mid = pl.ds(Y0, PY)
        v, t = beside_sum(p, x, Y0, PY)
        return v, [fo[h, x, mid] - dg[h, x, mid] * v[h] + t[h] for h in range(2)]

    planes(X0 - 1, X0 + PX + 1, sweep(pa, pb))

    def restrict(i, carry):
        a = X0 + 2 * i
        va, ra = residual(pb, a)
        vb, rb = residual(pb, a + 1)
        dst = pl.ds(pl.multiple_of(i * CY, CY), CY)
        for h in range(2):
            pc[h, a, pl.ds(Y0, PY)] = va[h]
            pc[h, a + 1, pl.ds(Y0, PY)] = vb[h]
            ybuf[h] = ra[h] + rb[h]
            zbuf[4, dst, pl.ds(h * LANES, LANES)] = (
                ybuf[h, pl.ds(0, CY, stride=2)] + ybuf[h, pl.ds(1, CY, stride=2)]
            )
        return carry

    lax.fori_loop(0, CX, restrict, 0)
    rem[own] = zdot(zbuf[4], both).reshape(cube)
    rem_start()
    p_start()

    cw_recv()
    theta = (UPPER + LOWER) / 2.0
    delta = (UPPER - LOWER) / 2.0
    ratio = delta / theta

    def invert(x):
        r = pl.ds(1, GY - 2)
        c = cw[3, x, r]
        cinv[x, r] = jnp.where(c > 0.0, 1.0 / jnp.where(c > 0.0, c, 1.0), 0.0)

    planes(0, GX, invert)
    rem_recv()
    rem_sent()

    def first_heading(x):
        r = pl.ds(1, GY - 2)
        heading = rem[x, r] * cinv[x, r] * (1.0 / theta)
        ha[x, r] = heading
        cor[x, r] = heading

    planes(0, GX, first_heading)

    def coarse_step(old, new, r0, n, keep, add):
        mid, above, below = pl.ds(r0, n), pl.ds(r0 + 1, n), pl.ds(r0 - 1, n)

        def body(x):
            v = old[x, mid]
            u = cw[2, x, mid]
            t = cw[0, x, mid] * old[x + 1, mid] + cw[0, x - 1, mid] * old[x - 1, mid]
            t = t + cw[1, x, mid] * old[x, above] + cw[1, x, below] * old[x, below]
            t = t + u * pltpu.roll(v, LANES - 1, 1) + pltpu.roll(u * v, 1, 1)
            left = rem[x, mid] - (cw[3, x, mid] * v - t)
            rem[x, mid] = left
            heading = keep * v + add * (left * cinv[x, mid])
            new[x, mid] = heading
            cor[x, mid] = cor[x, mid] + heading

        return body

    old, new = ha, hb
    for turn in range(1, CHEB):
        following = 1.0 / (2.0 * theta / delta - ratio)
        halo = CW - turn
        n = -(-(CY + 2 * halo) // 8) * 8
        n = min(n, GY - 2 * (CY0 - halo))
        planes(
            CX0 - halo,
            CX0 + CX + halo,
            coarse_step(old, new, CY0 - halo, n, following * ratio, 2.0 * following / delta),
        )
        ratio = following
        old, new = new, old

    zi = lax.broadcasted_iota(jnp.int32, (LANES, 2 * LANES), 0)
    zo = lax.broadcasted_iota(jnp.int32, (LANES, 2 * LANES), 1)
    spread = jnp.where(zo // 2 == zi, 1.0, 0.0).astype(jnp.bfloat16)
    p_recv()

    def prolong(c):
        wide = zdot(cor[c, pl.ds(CY0 - 2, CY + 8)], spread)
        x = 2 * (c - CX0) + X0
        for h in range(2):
            part_h = wide[: CY + 4, h * LANES : (h + 1) * LANES]
            ebuf[h, pl.ds(R0, RN // 2, stride=2)] = part_h
            ebuf[h, pl.ds(R0 + 1, RN // 2, stride=2)] = part_h
            for k in range(2):
                pc[h, x + k, rows] = pc[h, x + k, rows] + ebuf[h, rows]

    planes(CX0 - 2, CX0 + CX + 2, prolong)
    planes(X0 - W + 1, X0 + PX + W - 1, sweep(pc, pa))
    p_sent()
    planes(X0 - 1, X0 + PX + 1, sweep(pa, pb))

    def stores(ref, off, hbm, sem):
        return [
            pltpu.make_async_copy(
                ref.at[h, pl.ds(off[0], PX), pl.ds(off[1], PY)],
                hbm.at[:, :, pl.ds(h * LANES, LANES)],
                sem.at[h],
            )
            for h in range(2)
        ]

    store_p = stores(pb, (X0, Y0), out_p, out_sem.at[0])
    store_r = stores(res, (0, 0), out_r, out_sem.at[1])
    for copy in store_p:
        copy.start()

    def last(x):
        _, r = residual(pb, x)
        for h in range(2):
            res[h, x - X0] = r[h]

    planes(X0, X0 + PX, last)
    for copy in store_r:
        copy.start()
    ph_sent()
    src_sent()
    cw_sent()
    for copy in store_p + store_r:
        copy.wait()


def per_device(source, phases):
    ns, ng = lax.axis_size("space"), lax.axis_size("group")
    fine = (2, FX, FY, LANES)
    coarse = (GX, GY, LANES)
    flat = CX * CY
    vmem = pltpu.VMEM
    scratch = [vmem(fine, jnp.int32)]
    scratch += [vmem(fine, F32)] * 11
    scratch += [vmem((2, PX, PY, LANES), F32), vmem((4,) + coarse, F32)]
    scratch += [vmem(coarse, F32)] * 5
    scratch += [
        vmem((5, flat, 2 * LANES), F32),
        vmem((2, PY, LANES), F32),
        vmem((2, FY, LANES), F32),
        vmem((2, 1, LANES), F32),
        vmem((4 * ng, 1, LANES), F32),
        vmem((ns // 4, 1, LANES), F32),
        pltpu.SemaphoreType.DMA((2, 2)),
        pltpu.SemaphoreType.DMA((2, 2)),
        pltpu.SemaphoreType.DMA((2,)),
        pltpu.SemaphoreType.DMA((2,)),
        pltpu.SemaphoreType.DMA((5, len(DIRS))),
        pltpu.SemaphoreType.DMA((5, len(DIRS))),
    ]
    return pl.pallas_call(
        functools.partial(kernel, ns, ng),
        out_shape=[jax.ShapeDtypeStruct(source.shape, F32)] * 2,
        in_specs=[pl.BlockSpec(memory_space=pl.ANY)] * 2,
        out_specs=[pl.BlockSpec(memory_space=pl.ANY)] * 2,
        scratch_shapes=scratch,
        compiler_params=pltpu.CompilerParams(
            collective_id=0, has_side_effects=True, vmem_limit_bytes=56 * 2**20
        ),
    )(source, phases)


def solution(mesh):
    spec = P("space", "group", None)
    return jax.shard_map(
        per_device, mesh=mesh, in_specs=(spec, spec), out_specs=(spec, spec), check_vma=False
    )
```

```python
import functools
import math

import jax
import jax.numpy as jnp
from jax import lax
from jax.experimental import pallas as pl
from jax.experimental.pallas import tpu as pltpu
from jax.sharding import PartitionSpec as P

CHEB = 6
PHASES = 8
REACTION = 0.01
RELAX = 0.8
LOWER = 0.05
UPPER = 2.0

F32 = jnp.float32
MESH = pl.DeviceIdType.MESH

PX, PY, LANES = 16, 64, 128
X0, Y0 = 4, 8
FX, FY = PX + 2 * X0, PY + 2 * Y0
W = 3
R0, RN = 4, 72
CX, CY = PX // 2, PY // 2
CW, CX0, CY0 = 7, 7, 8
GX, GY = CX + 2 * CX0, CY + 2 * CY0
DIRS = [(-1, 0), (1, 0), (0, -1), (0, 1), (-1, -1), (-1, 1), (1, -1), (1, 1)]
MESSAGES = 8 * 3 + 16 + 4 + 12
NO_CELL = 1 << 20
NEAR, NEAR_ROWS, FAR_ROWS = 3, 6, 3


def spans(step, start, size, near, far):
    if step == 0:
        return pl.ds(start, size), pl.ds(start, size)
    width = far - near
    if step > 0:
        return pl.ds(start + size - far, width), pl.ds(start - far, width)
    return pl.ds(start + near, width), pl.ds(start + size + near, width)


def harmonic(left, right):
    return 2.0 * left * right / jnp.maximum(left + right, 1e-30)


def zdot(x, matrix):
    high = x.astype(jnp.bfloat16)
    rest = x - high.astype(F32)
    mid = rest.astype(jnp.bfloat16)
    low = (rest - mid.astype(F32)).astype(jnp.bfloat16)
    dot = functools.partial(jnp.dot, preferred_element_type=F32)
    return dot(high, matrix) + dot(mid, matrix) + dot(low, matrix)


def lane_map(rows, cols, place):
    i = lax.broadcasted_iota(jnp.int32, (rows, cols), 0)
    o = lax.broadcasted_iota(jnp.int32, (rows, cols), 1)
    return jnp.where(place(i, o), 1.0, 0.0).astype(jnp.bfloat16)


def planes(lo, hi, body, k=1):
    def run(first, count):
        stores = [store for j in range(count) for store in body(first + j, j)]
        for ref, at, value in stores:
            ref[at] = value

    def step(j, carry):
        run(lo + j * k, k)
        return carry

    whole = (hi - lo) // k
    lax.fori_loop(0, whole, step, 0)
    if (hi - lo) % k:
        run(lo + whole * k, (hi - lo) % k)


def kernel(
    ns, ng, source_hbm, phases_hbm, out_p, out_r,
    ph, src, kap, wx, wy, wz, dg, di, fo, pa, pb, pc,
    cw, rem, cinv, ha, hb, cor, eb, nb, zbuf, ybuf, ebuf, wide,
    part, sum1, sum2,
    in_sem, psend, precv, send, recv,
):
    s, g = lax.axis_index("space"), lax.axis_index("group")
    lane = lax.broadcasted_iota(jnp.int32, (1, LANES), 1)
    first, last = lane == 0, lane == LANES - 1

    def here(dx, dy):
        ok = jnp.bool_(True)
        if dx < 0:
            ok = s > 0
        if dx > 0:
            ok = s < ns - 1
        if dy < 0:
            ok = jnp.logical_and(ok, g > 0)
        if dy > 0:
            ok = jnp.logical_and(ok, g < ng - 1)
        return ok

    def halves(hbm, ref, sem):
        return [
            pltpu.make_async_copy(
                hbm.at[:, :, pl.ds(h * LANES, LANES)],
                ref.at[h, pl.ds(X0, PX), pl.ds(Y0, PY)],
                sem.at[h],
            )
            for h in range(2)
        ]

    load_ph = halves(phases_hbm, ph, in_sem.at[0])
    load_src = halves(source_hbm, src, in_sem.at[1])
    for copy in load_ph + load_src:
        copy.start()

    x4, q = lax.rem(s, 4), s // 4
    nq = ns // 4
    n1 = 4 * ng
    me1 = x4 * ng + g

    def peer1(j):
        t = lax.rem(me1 + j, n1)
        return (q * 4 + t // ng, lax.rem(t, ng))

    def peer2(j):
        return (lax.rem(q + j, nq) * 4 + x4, g)

    barrier = pltpu.get_barrier_semaphore()
    expected = jnp.int32(n1 - 1 + nq - 1)

    def greet(peer):
        pl.semaphore_signal(barrier, inc=1, device_id=peer, device_id_type=MESH)

    for j in range(1, n1):
        greet(peer1(j))
    for j in range(1, nq):
        greet(peer2(j))
    for dx, dy in DIRS:
        ok = here(dx, dy)

        @pl.when(ok)
        def _():
            greet((s + dx, g + dy))

        expected = expected + ok.astype(jnp.int32)

    used = [0]

    def exchange(messages):
        base = used[0]
        used[0] += len(messages)

        def copy(k):
            (dx, dy), source, target = messages[k]
            return pltpu.make_async_remote_copy(
                src_ref=source,
                dst_ref=target,
                send_sem=send.at[base + k],
                recv_sem=recv.at[base + k],
                device_id=(s + dx, g + dy),
                device_id_type=MESH,
            )

        def each(sign, act):
            for k, ((dx, dy), _, _) in enumerate(messages):

                @pl.when(here(sign * dx, sign * dy))
                def _():
                    act(copy(k))

        return (
            lambda: each(1, lambda c: c.start()),
            lambda: each(-1, lambda c: c.wait_recv()),
            lambda: each(1, lambda c: c.wait_send()),
        )

    def fill(messages, value):
        for (dx, dy), _, target in messages:

            @pl.when(jnp.logical_not(here(-dx, -dy)))
            def _():
                target[...] = jnp.full(target.shape, value, target.dtype)

    def fine_messages(a, b, width, skip=0):
        messages = []
        for dx, dy in DIRS:
            reach = width - 1 if dx and dy else width
            sx, tx = spans(dx, X0, PX, 0 if dy else skip, reach)
            sy, ty = spans(dy, Y0, PY, 0, reach)
            messages.append(((dx, dy), a.at[:, sx, sy], b.at[:, tx, ty]))
        return messages

    def coarse_messages(a, parts):
        messages = []
        for dx, dy in DIRS:
            if dx and dy:
                boxes = [(0, NEAR, NEAR_ROWS, None), (NEAR, CW - 1, FAR_ROWS, None)]
            else:
                boxes = [(0, far, CW, span) for span, far in parts or [(None, CW)]]
            for near, far, count, span in boxes:
                sx, tx = spans(dx, CX0, CX, near, far)
                sy, ty = spans(dy, CY0, CY, 0, count)
                lead = () if parts is None else (span or slice(None),)
                messages.append(((dx, dy), a.at[lead + (sx, sy)], a.at[lead + (tx, ty)]))
        return messages

    ph_all = fine_messages(ph, ph, W)
    src_all = fine_messages(src, src, W - 1)
    p_all = fine_messages(pb, pc, W, 1)
    cw_all = coarse_messages(cw, [(pl.ds(0, 2), CW), (pl.ds(2, 2), CW - 1)])
    rem_all = coarse_messages(rem, None)
    rim_all = []
    for d in (-1, 1):
        sx, tx = spans(d, CX0, CX, 0, CW)
        sy, ty = spans(d, CY0, CY, 0, CW)
        rim_all.append(((d, 0), nb.at[sx], nb.at[tx]))
        rim_all.append(((0, d), eb.at[:, sy], eb.at[:, ty]))
    fill(fine_messages(ph, ph, W), NO_CELL)
    for messages in (src_all, p_all, cw_all, rem_all, rim_all):
        fill(messages, 0)
    ph_start, ph_recv, ph_sent = exchange(ph_all)
    src_start, src_recv, src_sent = exchange(src_all)
    cw_start, cw_recv, cw_sent = exchange(cw_all)
    rim_start, rim_recv, rim_sent = exchange(rim_all)
    rem_start, rem_recv, rem_sent = exchange(rem_all)
    p_start, p_recv, p_sent = exchange(p_all)

    def conductivity(x, r0, n):
        at = pl.ds(r0, n)
        rate = -6.0 * math.log(10.0) / (PHASES - 1)
        return [(kap, (h, x, at), jnp.exp(ph[h, x, at].astype(F32) * rate)) for h in range(2)]

    def faces(x, r0, n):
        rows, above = pl.ds(r0, n), pl.ds(r0 + 1, n)
        k = [kap[h, x, rows] for h in range(2)]
        up = [pltpu.roll(k[h], LANES - 1, 1) for h in range(2)]
        beside = [jnp.where(last, up[1], up[0]), jnp.where(last, 0.0, up[1])]
        stores = []
        for h in range(2):
            stores.append((wx, (h, x, rows), harmonic(k[h], kap[h, x + 1, rows])))
            stores.append((wy, (h, x, rows), harmonic(k[h], kap[h, x, above])))
            stores.append((wz, (h, x, rows), harmonic(k[h], beside[h])))
        return stores

    def diagonal(x, r0, n):
        rows, below = pl.ds(r0, n), pl.ds(r0 - 1, n)
        z = [wz[h, x, rows] for h in range(2)]
        down = [pltpu.roll(z[h], 1, 1) for h in range(2)]
        beside = [jnp.where(first, 0.0, down[0]), jnp.where(first, down[0], down[1])]
        stores = []
        for h in range(2):
            d = REACTION * kap[h, x, rows] + wx[h, x, rows] + wx[h, x - 1, rows]
            d = d + wy[h, x, rows] + wy[h, x, below] + z[h] + beside[h]
            stores.append((dg, (h, x, rows), d))
            scaled = jnp.where(d > 0.0, RELAX / jnp.where(d > 0.0, d, 1.0), 0.0)
            stores.append((di, (h, x, rows), scaled))
        return stores

    def zero(ref, at):
        ref[at] = jnp.zeros(ref.at[at].shape, F32)

    for copy in load_ph:
        copy.wait()
    planes(X0, X0 + PX, lambda x, _: conductivity(x, Y0, PY), 2)
    both_h = pl.ds(0, 2)
    zero(kap, (both_h, X0 + PX, pl.ds(Y0, PY)))
    zero(wx, (both_h, X0 - 1, pl.ds(Y0, PY)))
    zero(kap, (both_h, pl.ds(X0, PX), pl.ds(Y0 + PY, 8)))
    zero(wy, (both_h, pl.ds(X0, PX), pl.ds(0, Y0)))

    for copy in load_src:
        copy.wait()

    def add_plane(x, total):
        plane = src[0, x, pl.ds(Y0, PY)] + src[1, x, pl.ds(Y0, PY)]
        return total + jnp.sum(plane.reshape(PY // 8, 8, LANES), axis=0)

    local = lax.fori_loop(X0, X0 + PX, add_plane, jnp.zeros((8, LANES), F32))
    local = jnp.sum(local, axis=0, keepdims=True)
    part[0] = local
    sum1[me1] = local

    pl.semaphore_wait(barrier, expected)

    def gather_part(stage, slots, count, me, peer):
        def start():
            for j in range(1, count):
                pltpu.make_async_remote_copy(
                    src_ref=part.at[stage],
                    dst_ref=slots.at[me],
                    send_sem=psend.at[stage],
                    recv_sem=precv.at[stage],
                    device_id=peer(j),
                    device_id_type=MESH,
                ).start()

        def wait():
            pltpu.make_async_remote_copy(
                src_ref=slots.at[pl.ds(0, count - 1)],
                dst_ref=slots.at[pl.ds(0, count - 1)],
                send_sem=psend.at[stage],
                recv_sem=precv.at[stage],
                device_id=peer(1),
                device_id_type=MESH,
            ).wait()

        return start, wait

    start1, wait1 = gather_part(0, sum1, n1, me1, peer1)
    start2, wait2 = gather_part(1, sum2, nq, q, peer2)
    start1()
    ph_start()
    src_start()

    planes(X0, X0 + PX, lambda x, _: faces(x, Y0, PY), 2)

    both = lane_map(2 * LANES, LANES, lambda i, o: i // 2 == o)
    upper = lane_map(2 * LANES, LANES, lambda i, o: i == 2 * o + 1)
    outer = lane_map(2 * LANES, LANES, lambda i, o: (i == 2 * o + 1) | (i == 2 * o - 1))
    even, odd = pl.ds(Y0, CY, stride=2), pl.ds(Y0 + 1, CY, stride=2)
    under = pl.ds(Y0 - 1, CY, stride=2)

    def pair(ref, h, x):
        return ref[h, x, even] + ref[h, x, odd]

    def coarse_parts(i, _):
        a = X0 + 2 * i
        b = a + 1
        rows = pl.ds(pl.multiple_of(i * CY, CY), CY)
        stores = []
        for h in range(2):
            cols = pl.ds(h * LANES, LANES)
            east = pair(wx, h, b)
            north = wy[h, a, odd] + wy[h, b, odd]
            south = wy[h, a, under] + wy[h, b, under]
            kept = REACTION * (pair(kap, h, a) + pair(kap, h, b))
            middle = kept + east + pair(wx, h, a - 1) + north + south
            for k, value in enumerate((middle, east, north, pair(wz, h, a) + pair(wz, h, b))):
                stores.append((zbuf, (k, rows, cols), value))
        return stores

    planes(0, CX, coarse_parts, 2)

    own = (pl.ds(CX0, CX), pl.ds(CY0, CY))
    cube = (CX, CY, LANES)
    cw[(0,) + own] = (zdot(zbuf[0], both) + zdot(zbuf[3], outer)).reshape(cube)
    cw[(1,) + own] = zdot(zbuf[1], both).reshape(cube)
    cw[(2,) + own] = zdot(zbuf[2], both).reshape(cube)
    cw[(3,) + own] = zdot(zbuf[3], upper).reshape(cube)
    wait1()
    total1 = jnp.sum(sum1[...], axis=0)
    part[1] = total1
    sum2[q] = total1
    start2()

    planes(X0 + 1, X0 + PX - 1, lambda x, _: diagonal(x, Y0, PY), 2)

    ph_recv()

    def sides(body, lo, hi):
        def both_sides(x, _):
            return body(x, lo, 8) + body(x, hi, 8)

        return both_sides

    planes(X0, X0 + PX, sides(conductivity, 0, FY - 8), 4)
    for lo in (X0 - W, X0 + PX):
        planes(lo, lo + W, lambda x, _: conductivity(x, 0, FY), 3)
    for lo, hi in ((X0 - W, X0 + 1), (X0 + PX - 1, X0 + PX + W - 1)):
        planes(lo, hi, lambda x, _: faces(x, R0, RN), 2)
    planes(X0 + 1, X0 + PX - 1, sides(faces, R0, R0 + RN - 8), 7)

    zbuf[4, pl.ds(0, CY)] = jnp.concatenate([pair(wx, h, X0 - 1) for h in range(2)], axis=1)
    zbuf[4, pl.ds(CY, CY)] = jnp.concatenate([pair(wx, h, X0 + PX - 1) for h in range(2)], axis=1)
    for i in range(CX):
        for k, row in enumerate((Y0 - 1, Y0 + PY - 1)):
            for h in range(2):
                zbuf[4, pl.ds(2 * CY + k * CX + i, 1), pl.ds(h * LANES, LANES)] = (
                    wy[h, X0 + 2 * i, pl.ds(row, 1)] + wy[h, X0 + 2 * i + 1, pl.ds(row, 1)]
                )
    rim = zdot(zbuf[4, pl.ds(0, 2 * CY + 2 * CX)], both)
    eb[0, pl.ds(CY0, CY)] = rim[:CY]
    eb[1, pl.ds(CY0, CY)] = rim[CY : 2 * CY]
    for i in range(CX):
        for k in range(2):
            j = 2 * CY + k * CX + i
            nb[CX0 + i, pl.ds(k, 1)] = rim[j : j + 1]
    rim_start()

    for lo, hi in ((X0 - W + 1, X0 + 1), (X0 + PX - 1, X0 + PX + W - 1)):
        planes(lo, hi, lambda x, _: diagonal(x, R0, RN), 3)
    planes(X0 + 1, X0 + PX - 1, sides(diagonal, R0, R0 + RN - 8), 7)

    wait2()
    total = jnp.sum(sum2[...], axis=0)
    average = jnp.sum(total, axis=1, keepdims=True) * (1.0 / (PX * ns * PY * ng * 2 * LANES))
    src_recv()
    cw_start()

    rows = pl.ds(R0, RN)

    def first_sweep(x, _):
        stores = []
        for h in range(2):
            f = kap[h, x, rows] * (src[h, x, rows] - average)
            stores.append((fo, (h, x, rows), f))
            stores.append((pa, (h, x, rows), di[h, x, rows] * f))
        return stores

    planes(X0 - W + 1, X0 + PX + W - 1, first_sweep, 2)

    def beside_sum(p, x, r0, n):
        mid, above, below = pl.ds(r0, n), pl.ds(r0 + 1, n), pl.ds(r0 - 1, n)
        v = [p[h, x, mid] for h in range(2)]
        z = [wz[h, x, mid] for h in range(2)]
        up = [pltpu.roll(v[h], LANES - 1, 1) for h in range(2)]
        down = [pltpu.roll(z[h] * v[h], 1, 1) for h in range(2)]
        up[0] = jnp.where(last, up[1], up[0])
        down = [jnp.where(first, 0.0, down[0]), jnp.where(first, down[0], down[1])]
        sums = []
        for h in range(2):
            t = wx[h, x, mid] * p[h, x + 1, mid] + wx[h, x - 1, mid] * p[h, x - 1, mid]
            t = t + wy[h, x, mid] * p[h, x, above] + wy[h, x, below] * p[h, x, below]
            sums.append(t + z[h] * up[h] + down[h])
        return v, sums

    def sweep(old, new):
        def body(x, _):
            v, t = beside_sum(old, x, R0, RN)
            return [
                (new, (h, x, rows), (1.0 - RELAX) * v[h] + di[h, x, rows] * (fo[h, x, rows] + t[h]))
                for h in range(2)
            ]

        return body

    mid = pl.ds(Y0, PY)

    def residual(p, x):
        v, t = beside_sum(p, x, Y0, PY)
        return v, [fo[h, x, mid] - dg[h, x, mid] * v[h] + t[h] for h in range(2)]

    planes(X0 - 1, X0 + PX + 1, sweep(pa, pb), 2)

    def restrict(i, slot):
        a = X0 + 2 * i
        va, ra = residual(pb, a)
        vb, rb = residual(pb, a + 1)
        dst = pl.ds(pl.multiple_of(i * CY, CY), CY)
        stores = []
        for h in range(2):
            stores.append((pc, (h, a, mid), va[h]))
            stores.append((pc, (h, a + 1, mid), vb[h]))
            ybuf[slot, h] = ra[h] + rb[h]
            halves_y = ybuf[slot, h, pl.ds(0, CY, stride=2)] + ybuf[slot, h, pl.ds(1, CY, stride=2)]
            stores.append((zbuf, (4, dst, pl.ds(h * LANES, LANES)), halves_y))
        return stores

    planes(0, CX, restrict, 2)
    rem[own] = zdot(zbuf[4], both).reshape(cube)
    rem_start()
    p_start()
    for x in (X0 - 1, X0 + PX):
        pc[:, x, mid] = pb[:, x, mid]

    theta = (UPPER + LOWER) / 2.0
    delta = (UPPER - LOWER) / 2.0
    ratio = delta / theta
    cw_recv()
    cw_sent()
    rim_recv()
    body_rows = pl.ds(1, GY - 2)
    for k, x in enumerate((CX0 - 1, CX0 + CX - 1)):
        east = eb[k, body_rows]
        cw[1, x, body_rows] = east
        for j in (x, x + 1):
            cw[0, j, body_rows] = cw[0, j, body_rows] + east

    def rim_rows(x, _):
        stores = []
        for k, r in enumerate((CY0 - 1, CY0 + CY - 1)):
            north = nb[x, pl.ds(k, 1)]
            stores.append((cw, (2, x, pl.ds(r, 1)), north))
            for j in (r, r + 1):
                stores.append((cw, (0, x, pl.ds(j, 1)), cw[0, x, pl.ds(j, 1)] + north))
        return stores

    planes(0, GX, rim_rows, 2)

    def invert(x, _):
        c = cw[0, x, body_rows]
        c = jnp.where(c > 0.0, 1.0 / jnp.where(c > 0.0, c, 1.0), 0.0)
        return [(cinv, (x, body_rows), c)]

    planes(0, GX, invert, 2)
    rem_recv()
    rem_sent()

    def first_heading(x, _):
        heading = rem[x, body_rows] * cinv[x, body_rows] * (1.0 / theta)
        return [(ha, (x, body_rows), heading), (cor, (x, body_rows), heading)]

    planes(0, GX, first_heading, 2)

    def coarse_step(old, new, r0, n, keep, add):
        mid, above, below = pl.ds(r0, n), pl.ds(r0 + 1, n), pl.ds(r0 - 1, n)

        def body(x, _):
            v = old[x, mid]
            u = cw[3, x, mid]
            t = cw[1, x, mid] * old[x + 1, mid] + cw[1, x - 1, mid] * old[x - 1, mid]
            t = t + cw[2, x, mid] * old[x, above] + cw[2, x, below] * old[x, below]
            t = t + u * pltpu.roll(v, LANES - 1, 1) + pltpu.roll(u * v, 1, 1)
            left = rem[x, mid] - (cw[0, x, mid] * v - t)
            heading = keep * v + add * (left * cinv[x, mid])
            return [
                (rem, (x, mid), left),
                (new, (x, mid), heading),
                (cor, (x, mid), cor[x, mid] + heading),
            ]

        return body

    old, new = ha, hb
    for turn in range(1, CHEB):
        following = 1.0 / (2.0 * theta / delta - ratio)
        halo = CW - turn
        lo, hi = CX0 - halo, CX0 + CX + halo
        step = coarse_step(
            old, new, CY0 - halo, CY + 2 * halo, following * ratio, 2.0 * following / delta
        )
        planes(lo, hi, step, {20: 5, 18: 6, 16: 4, 14: 7, 12: 6}[hi - lo])
        ratio = following
        old, new = new, old

    spread = lane_map(LANES, 2 * LANES, lambda i, o: o // 2 == i)
    top = CX + 4
    picked = cor[pl.ds(CX0 - 2, top), pl.ds(CY0 - 2, CY + 8)]
    wide[...] = zdot(picked.reshape(top * (CY + 8), LANES), spread)
    p_recv()

    def prolong(c, slot):
        x = 2 * c + X0 - 4
        stores = []
        for h in range(2):
            part_h = wide[pl.ds(pl.multiple_of(c * (CY + 8), 8), CY + 4), pl.ds(h * LANES, LANES)]
            ebuf[slot, h, pl.ds(R0, RN // 2, stride=2)] = part_h
            ebuf[slot, h, pl.ds(R0 + 1, RN // 2, stride=2)] = part_h
            for k in range(2):
                stores.append((pc, (h, x + k, rows), pc[h, x + k, rows] + ebuf[slot, h, rows]))
        return stores

    planes(0, top, prolong, 2)
    planes(X0 - W + 1, X0 + PX + W - 1, sweep(pc, pa), 2)
    p_sent()
    planes(X0 - 1, X0 + PX + 1, sweep(pa, pb), 2)

    def finish(x, _):
        v, r = residual(pb, x)
        stores = []
        for h in range(2):
            at = (x - X0, pl.ds(0, PY), pl.ds(h * LANES, LANES))
            stores += [(out_p, at, v[h]), (out_r, at, r[h])]
        return stores

    planes(X0, X0 + PX, finish, 2)
    ph_sent()
    src_sent()
    rim_sent()


def write_out(p, r, out_p, out_r, sem):
    copies = [pltpu.make_async_copy(p, out_p, sem.at[0]), pltpu.make_async_copy(r, out_r, sem.at[1])]
    for copy in copies:
        copy.start()
    for copy in copies:
        copy.wait()


def per_device(source, phases):
    ns, ng = lax.axis_size("space"), lax.axis_size("group")
    fine = (2, FX, FY, LANES)
    coarse = (GX, GY, LANES)
    flat = CX * CY
    vmem = pltpu.VMEM
    scratch = [vmem(fine, jnp.int32)]
    scratch += [vmem(fine, F32)] * 11
    scratch += [vmem((4,) + coarse, F32)]
    scratch += [vmem(coarse, F32)] * 5
    scratch += [
        vmem((2, GY, LANES), F32),
        vmem((GX, 2, LANES), F32),
        vmem((5, flat, 2 * LANES), F32),
        vmem((2, 2, PY, LANES), F32),
        vmem((2, 2, FY, LANES), F32),
        vmem(((CX + 4) * (CY + 8), 2 * LANES), F32),
        vmem((2, 1, LANES), F32),
        vmem((4 * ng, 1, LANES), F32),
        vmem((ns // 4, 1, LANES), F32),
        pltpu.SemaphoreType.DMA((2, 2)),
        pltpu.SemaphoreType.DMA((2,)),
        pltpu.SemaphoreType.DMA((2,)),
        pltpu.SemaphoreType.DMA((MESSAGES,)),
        pltpu.SemaphoreType.DMA((MESSAGES,)),
    ]
    out_shape = [jax.ShapeDtypeStruct(source.shape, F32)] * 2
    pressure, residual = pl.pallas_call(
        functools.partial(kernel, ns, ng),
        out_shape=out_shape,
        in_specs=[pl.BlockSpec(memory_space=pltpu.HBM)] * 2,
        out_specs=[pl.BlockSpec(memory_space=pltpu.VMEM)] * 2,
        scratch_shapes=scratch,
        compiler_params=pltpu.CompilerParams(
            collective_id=0, has_side_effects=True, vmem_limit_bytes=40 * 2**20
        ),
    )(source, phases)
    return pl.pallas_call(
        write_out,
        out_shape=out_shape,
        in_specs=[pl.BlockSpec(memory_space=pl.ANY)] * 2,
        out_specs=[pl.BlockSpec(memory_space=pl.ANY)] * 2,
        scratch_shapes=[pltpu.SemaphoreType.DMA((2,))],
        compiler_params=pltpu.CompilerParams(vmem_limit_bytes=2**20),
    )(pressure, residual)


def solution(mesh):
    spec = P("space", "group", None)
    return jax.shard_map(
        per_device, mesh=mesh, in_specs=(spec, spec), out_specs=(spec, spec), check_vma=False
    )
```

```python
import functools
import math

import jax
import jax.numpy as jnp
from jax import lax
from jax.experimental import pallas as pl
from jax.experimental.pallas import tpu as pltpu
from jax.sharding import PartitionSpec as P

CHEB = 6
PHASES = 8
REACTION = 0.01
RELAX = 0.8
LOWER = 0.05
UPPER = 2.0

F32 = jnp.float32
MESH = pl.DeviceIdType.MESH

PX, PY, LANES = 16, 64, 128
X0, Y0 = 4, 8
FX, FY = PX + 2 * X0, PY + 2 * Y0
W = 3
R0, RN = 4, 72
CX, CY = PX // 2, PY // 2
CW, CX0, CY0 = 7, 7, 8
GX, GY = CX + 2 * CX0, CY + 2 * CY0
CS = CY + 8
DIRS = [(-1, 0), (1, 0), (0, -1), (0, 1), (-1, -1), (-1, 1), (1, -1), (1, 1)]
MESSAGES = 8 * 4 + 16 + 12
NO_CELL = 1 << 20
NEAR, NEAR_ROWS, FAR_ROWS = 3, 6, 3


def spans(step, start, size, near, far):
    if step == 0:
        return pl.ds(start, size), pl.ds(start, size)
    width = far - near
    if step > 0:
        return pl.ds(start + size - far, width), pl.ds(start - far, width)
    return pl.ds(start + near, width), pl.ds(start + size + near, width)


def harmonic(left, right):
    return 2.0 * left * right / jnp.maximum(left + right, 1e-30)


def zdot(x, matrix):
    high = x.astype(jnp.bfloat16)
    rest = x - high.astype(F32)
    mid = rest.astype(jnp.bfloat16)
    low = (rest - mid.astype(F32)).astype(jnp.bfloat16)
    dot = functools.partial(jnp.dot, preferred_element_type=F32)
    return dot(high, matrix) + dot(mid, matrix) + dot(low, matrix)


def lane_map(rows, cols, place):
    i = lax.broadcasted_iota(jnp.int32, (rows, cols), 0)
    o = lax.broadcasted_iota(jnp.int32, (rows, cols), 1)
    return jnp.where(place(i, o), 1.0, 0.0).astype(jnp.bfloat16)


def planes(lo, hi, body, k=1):
    def run(first, count):
        stores = [store for j in range(count) for store in body(first + j, j)]
        for ref, at, value in stores:
            ref[at] = value

    def step(j, carry):
        run(lo + j * k, k)
        return carry

    whole = (hi - lo) // k
    lax.fori_loop(0, whole, step, 0)
    if (hi - lo) % k:
        run(lo + whole * k, (hi - lo) % k)


def kernel(
    ns, ng, source_hbm, phases_hbm, out_p, out_r,
    ph, src, kap, wx, wy, wz, dg, di, fo, pa, pb, pc,
    cw, cc, rem, ha, hb, cor, near, zbuf, ybuf, ebuf, wide,
    part, sum1, sum2,
    in_sem, psend, precv, send, recv,
):
    s, g = lax.axis_index("space"), lax.axis_index("group")
    lane = lax.broadcasted_iota(jnp.int32, (1, LANES), 1)
    first, last = lane == 0, lane == LANES - 1

    def here(dx, dy):
        ok = jnp.bool_(True)
        if dx < 0:
            ok = s > 0
        if dx > 0:
            ok = s < ns - 1
        if dy < 0:
            ok = jnp.logical_and(ok, g > 0)
        if dy > 0:
            ok = jnp.logical_and(ok, g < ng - 1)
        return ok

    def halves(hbm, ref, sem):
        return [
            pltpu.make_async_copy(
                hbm.at[:, :, pl.ds(h * LANES, LANES)],
                ref.at[h, pl.ds(X0, PX), pl.ds(Y0, PY)],
                sem.at[h],
            )
            for h in range(2)
        ]

    load_ph = halves(phases_hbm, ph, in_sem.at[0])
    load_src = halves(source_hbm, src, in_sem.at[1])
    for copy in load_ph + load_src:
        copy.start()

    x4, q = lax.rem(s, 4), s // 4
    nq = ns // 4
    n1 = 4 * ng
    me1 = x4 * ng + g

    def peer1(j):
        t = lax.rem(me1 + j, n1)
        return (q * 4 + t // ng, lax.rem(t, ng))

    def peer2(j):
        return (lax.rem(q + j, nq) * 4 + x4, g)

    barrier = pltpu.get_barrier_semaphore()
    expected = jnp.int32(n1 - 1 + nq - 1)

    def greet(peer):
        pl.semaphore_signal(barrier, inc=1, device_id=peer, device_id_type=MESH)

    for j in range(1, n1):
        greet(peer1(j))
    for j in range(1, nq):
        greet(peer2(j))
    for dx, dy in DIRS:
        ok = here(dx, dy)

        @pl.when(ok)
        def _():
            greet((s + dx, g + dy))

        expected = expected + ok.astype(jnp.int32)

    used = [0]

    def exchange(messages):
        base = used[0]
        used[0] += len(messages)

        def copy(k):
            (dx, dy), source, target = messages[k]
            return pltpu.make_async_remote_copy(
                src_ref=source,
                dst_ref=target,
                send_sem=send.at[base + k],
                recv_sem=recv.at[base + k],
                device_id=(s + dx, g + dy),
                device_id_type=MESH,
            )

        def each(sign, act):
            for k, ((dx, dy), _, _) in enumerate(messages):

                @pl.when(here(sign * dx, sign * dy))
                def _():
                    act(copy(k))

        return (
            lambda: each(1, lambda c: c.start()),
            lambda: each(-1, lambda c: c.wait_recv()),
            lambda: each(1, lambda c: c.wait_send()),
        )

    def fill(messages, value):
        for (dx, dy), _, target in messages:

            @pl.when(jnp.logical_not(here(-dx, -dy)))
            def _():
                target[...] = jnp.full(target.shape, value, target.dtype)

    def fine_messages(a, b, width, skip=0):
        messages = []
        for dx, dy in DIRS:
            reach = width - 1 if dx and dy else width
            sx, tx = spans(dx, X0, PX, 0 if dy else skip, reach)
            sy, ty = spans(dy, Y0, PY, 0, reach)
            messages.append(((dx, dy), a.at[:, sx, sy], b.at[:, tx, ty]))
        return messages

    def coarse_messages(a, parts):
        messages = []
        for dx, dy in DIRS:
            if dx and dy:
                boxes = [(0, NEAR, NEAR_ROWS, None), (NEAR, CW - 1, FAR_ROWS, None)]
            else:
                boxes = [(0, far, CW, span) for span, far in parts or [(None, CW)]]
            for near, far, count, span in boxes:
                sx, tx = spans(dx, CX0, CX, near, far)
                sy, ty = spans(dy, CY0, CY, 0, count)
                lead = () if parts is None else (span or slice(None),)
                messages.append(((dx, dy), a.at[lead + (sx, sy)], a.at[lead + (tx, ty)]))
        return messages

    ph_all = fine_messages(ph, ph, W)
    src_all = fine_messages(src, src, W - 1)
    p_all = fine_messages(pb, pc, W, 1)
    cw_all = coarse_messages(cw, [(pl.ds(0, 1), CW), (pl.ds(1, 2), CW - 1)])
    rem_all = coarse_messages(rem, None)
    near_all = []
    for dx, dy in DIRS:
        reach = 1 if dx and dy else 2
        sx, tx = spans(dx, CX0, CX, 0, reach)
        sy, ty = spans(dy, CY0, CY, 0, reach)
        near_all.append(((dx, dy), near.at[sx, sy], near.at[tx, ty]))
    fill(fine_messages(ph, ph, W), NO_CELL)
    for messages in (src_all, p_all, cw_all, rem_all, near_all):
        fill(messages, 0)
    ph_start, ph_recv, ph_sent = exchange(ph_all)
    src_start, src_recv, src_sent = exchange(src_all)
    cw_start, cw_recv, cw_sent = exchange(cw_all)
    rem_start, rem_recv, rem_sent = exchange(rem_all)
    p_start, p_recv, p_sent = exchange(p_all)
    near_start, near_recv, near_sent = exchange(near_all)

    def conductivity(x, r0, n):
        at = pl.ds(r0, n)
        rate = -6.0 * math.log(10.0) / (PHASES - 1)
        return [(kap, (h, x, at), jnp.exp(ph[h, x, at].astype(F32) * rate)) for h in range(2)]

    def faces(x, r0, n):
        rows, above = pl.ds(r0, n), pl.ds(r0 + 1, n)
        k = [kap[h, x, rows] for h in range(2)]
        up = [pltpu.roll(k[h], LANES - 1, 1) for h in range(2)]
        beside = [jnp.where(last, up[1], up[0]), jnp.where(last, 0.0, up[1])]
        stores = []
        for h in range(2):
            stores.append((wx, (h, x, rows), harmonic(k[h], kap[h, x + 1, rows])))
            stores.append((wy, (h, x, rows), harmonic(k[h], kap[h, x, above])))
            stores.append((wz, (h, x, rows), harmonic(k[h], beside[h])))
        return stores

    def diagonal(x, r0, n):
        rows, below = pl.ds(r0, n), pl.ds(r0 - 1, n)
        z = [wz[h, x, rows] for h in range(2)]
        down = [pltpu.roll(z[h], 1, 1) for h in range(2)]
        beside = [jnp.where(first, 0.0, down[0]), jnp.where(first, down[0], down[1])]
        stores = []
        for h in range(2):
            d = REACTION * kap[h, x, rows] + wx[h, x, rows] + wx[h, x - 1, rows]
            d = d + wy[h, x, rows] + wy[h, x, below] + z[h] + beside[h]
            stores.append((dg, (h, x, rows), d))
            scaled = jnp.where(d > 0.0, RELAX / jnp.where(d > 0.0, d, 1.0), 0.0)
            stores.append((di, (h, x, rows), scaled))
        return stores

    for copy in load_ph:
        copy.wait()
    planes(X0, X0 + PX, lambda x, _: conductivity(x, Y0, PY), 4)

    for copy in load_src:
        copy.wait()

    def add_plane(x, total):
        plane = src[0, x, pl.ds(Y0, PY)] + src[1, x, pl.ds(Y0, PY)]
        return total + jnp.sum(plane.reshape(PY // 8, 8, LANES), axis=0)

    local = lax.fori_loop(X0, X0 + PX, add_plane, jnp.zeros((8, LANES), F32))
    local = jnp.sum(local, axis=0, keepdims=True)
    part[0] = local
    sum1[me1] = local

    pl.semaphore_wait(barrier, expected)

    def gather_part(stage, slots, count, me, peer):
        def start():
            for j in range(1, count):
                pltpu.make_async_remote_copy(
                    src_ref=part.at[stage],
                    dst_ref=slots.at[me],
                    send_sem=psend.at[stage],
                    recv_sem=precv.at[stage],
                    device_id=peer(j),
                    device_id_type=MESH,
                ).start()

        def wait():
            pltpu.make_async_remote_copy(
                src_ref=slots.at[pl.ds(0, count - 1)],
                dst_ref=slots.at[pl.ds(0, count - 1)],
                send_sem=psend.at[stage],
                recv_sem=precv.at[stage],
                device_id=peer(1),
                device_id_type=MESH,
            ).wait()

        return start, wait

    start1, wait1 = gather_part(0, sum1, n1, me1, peer1)
    start2, wait2 = gather_part(1, sum2, nq, q, peer2)
    start1()
    ph_start()
    src_start()

    planes(X0, X0 + PX, lambda x, _: faces(x, Y0, PY), 4)

    wait1()
    total1 = jnp.sum(sum1[...], axis=0)
    part[1] = total1
    sum2[q] = total1
    start2()

    planes(X0 + 1, X0 + PX - 1, lambda x, _: diagonal(x, Y0, PY), 7)

    ph_recv()

    def sides(body, lo, hi):
        def both_sides(x, _):
            return body(x, lo, 8) + body(x, hi, 8)

        return both_sides

    planes(X0, X0 + PX, sides(conductivity, 0, FY - 8), 4)
    for lo in (X0 - W, X0 + PX):
        planes(lo, lo + W, lambda x, _: conductivity(x, 0, FY), 3)
    for lo, hi in ((X0 - W, X0 + 1), (X0 + PX - 1, X0 + PX + W - 1)):
        planes(lo, hi, lambda x, _: faces(x, R0, RN), 2)
    planes(X0 + 1, X0 + PX - 1, sides(faces, R0, R0 + RN - 8), 7)

    both = lane_map(2 * LANES, LANES, lambda i, o: i // 2 == o)
    upper = lane_map(2 * LANES, LANES, lambda i, o: i == 2 * o + 1)
    outer = lane_map(2 * LANES, LANES, lambda i, o: (i == 2 * o + 1) | (i == 2 * o - 1))
    even, odd = pl.ds(Y0, CY + 1, stride=2), pl.ds(Y0 + 1, CY + 1, stride=2)
    under = pl.ds(Y0 - 1, CY + 1, stride=2)

    def pair(ref, h, x):
        return ref[h, x, even] + ref[h, x, odd]

    def coarse_parts(i, _):
        a = X0 + 2 * i
        b = a + 1
        rows = pl.ds(pl.multiple_of(i * CS, 8), CY + 1)
        stores = []
        for h in range(2):
            cols = pl.ds(h * LANES, LANES)
            east = pair(wx, h, b)
            north = wy[h, a, odd] + wy[h, b, odd]
            south = wy[h, a, under] + wy[h, b, under]
            kept = REACTION * (pair(kap, h, a) + pair(kap, h, b))
            middle = kept + east + pair(wx, h, a - 1) + north + south
            for k, value in enumerate((middle, east, north, pair(wz, h, a) + pair(wz, h, b))):
                stores.append((zbuf, (k, rows, cols), value))
        return stores

    planes(0, CX + 1, coarse_parts, 3)

    flat = pl.ds(0, CX * CS)
    center = zdot(zbuf[0], both) + zdot(zbuf[3], outer)
    safe = jnp.where(center > 0.0, center, 1.0)
    d = lax.rsqrt(safe)
    d = jnp.where(center > 0.0, d * (1.5 - 0.5 * safe * d * d), 0.0)
    cc[...] = d.reshape(CX + 1, CS, LANES)
    weights = [zdot(zbuf[k, flat], m) for k, m in ((1, both), (2, both), (3, upper))]
    for k in range(3):
        zbuf[k, flat, pl.ds(0, LANES)] = weights[k]

    def scale(i, _):
        x = CX0 + i
        at, to = pl.ds(0, CY), pl.ds(CY0, CY)
        src_rows = pl.ds(pl.multiple_of(i * CS, 8), CY)
        mine = cc[i, at]
        beside = (cc[i + 1, at], cc[i, pl.ds(1, CY)], pltpu.roll(mine, LANES - 1, 1))
        stores = [(near, (x, to), mine)]
        for k in range(3):
            value = zbuf[k, src_rows, pl.ds(0, LANES)] * mine * beside[k]
            stores.append((cw, (k, x, to), value))
        return stores

    planes(0, CX, scale, 4)

    cw_start()

    for lo, hi in ((X0 - W + 1, X0 + 1), (X0 + PX - 1, X0 + PX + W - 1)):
        planes(lo, hi, lambda x, _: diagonal(x, R0, RN), 3)
    planes(X0 + 1, X0 + PX - 1, sides(diagonal, R0, R0 + RN - 8), 7)

    wait2()
    total = jnp.sum(sum2[...], axis=0)
    average = jnp.sum(total, axis=1, keepdims=True) * (1.0 / (PX * ns * PY * ng * 2 * LANES))
    src_recv()

    rows = pl.ds(R0, RN)

    def first_sweep(x, _):
        stores = []
        for h in range(2):
            f = kap[h, x, rows] * (src[h, x, rows] - average)
            stores.append((fo, (h, x, rows), f))
            stores.append((pa, (h, x, rows), di[h, x, rows] * f))
        return stores

    planes(X0 - W + 1, X0 + PX + W - 1, first_sweep, 4)

    def beside_sum(p, x, r0, n):
        mid, above, below = pl.ds(r0, n), pl.ds(r0 + 1, n), pl.ds(r0 - 1, n)
        v = [p[h, x, mid] for h in range(2)]
        z = [wz[h, x, mid] for h in range(2)]
        up = [pltpu.roll(v[h], LANES - 1, 1) for h in range(2)]
        down = [pltpu.roll(z[h] * v[h], 1, 1) for h in range(2)]
        up[0] = jnp.where(last, up[1], up[0])
        down = [jnp.where(first, 0.0, down[0]), jnp.where(first, down[0], down[1])]
        sums = []
        for h in range(2):
            t = wx[h, x, mid] * p[h, x + 1, mid] + wx[h, x - 1, mid] * p[h, x - 1, mid]
            t = t + wy[h, x, mid] * p[h, x, above] + wy[h, x, below] * p[h, x, below]
            sums.append(t + z[h] * up[h] + down[h])
        return v, sums

    def sweep(old, new):
        def body(x, _):
            v, t = beside_sum(old, x, R0, RN)
            return [
                (new, (h, x, rows), (1.0 - RELAX) * v[h] + di[h, x, rows] * (fo[h, x, rows] + t[h]))
                for h in range(2)
            ]

        return body

    mid = pl.ds(Y0, PY)

    def residual(p, x):
        v, t = beside_sum(p, x, Y0, PY)
        return v, [fo[h, x, mid] - dg[h, x, mid] * v[h] + t[h] for h in range(2)]

    planes(X0 - 1, X0 + PX + 1, sweep(pa, pb), 6)

    def restrict(i, slot):
        a = X0 + 2 * i
        va, ra = residual(pb, a)
        vb, rb = residual(pb, a + 1)
        dst = pl.ds(pl.multiple_of(i * CY, CY), CY)
        stores = []
        for h in range(2):
            stores.append((pc, (h, a, mid), va[h]))
            stores.append((pc, (h, a + 1, mid), vb[h]))
            ybuf[slot, h] = ra[h] + rb[h]
            halves_y = ybuf[slot, h, pl.ds(0, CY, stride=2)] + ybuf[slot, h, pl.ds(1, CY, stride=2)]
            stores.append((zbuf, (4, dst, pl.ds(h * LANES, LANES)), halves_y))
        return stores

    planes(0, CX, restrict, 4)
    coarse_forcing = zdot(zbuf[4, pl.ds(0, CX * CY)], both).reshape(CX, CY, LANES)
    rem[pl.ds(CX0, CX), pl.ds(CY0, CY)] = coarse_forcing * cc[pl.ds(0, CX), pl.ds(0, CY)]
    rem_start()
    p_start()
    near_start()
    for x in (X0 - 1, X0 + PX):
        pc[:, x, mid] = pb[:, x, mid]

    theta = (UPPER + LOWER) / 2.0
    delta = (UPPER - LOWER) / 2.0
    ratio = delta / theta
    body_rows = pl.ds(1, GY - 2)
    cw_recv()
    rem_recv()
    rem_sent()

    def first_heading(x, _):
        heading = rem[x, body_rows] * (1.0 / theta)
        return [(ha, (x, body_rows), heading), (cor, (x, body_rows), heading)]

    planes(0, GX, first_heading, 6)

    def coarse_step(old, new, r0, n, keep, add):
        mid, above, below = pl.ds(r0, n), pl.ds(r0 + 1, n), pl.ds(r0 - 1, n)

        def body(x, _):
            v = old[x, mid]
            u = cw[2, x, mid]
            t = cw[0, x, mid] * old[x + 1, mid] + cw[0, x - 1, mid] * old[x - 1, mid]
            t = t + cw[1, x, mid] * old[x, above] + cw[1, x, below] * old[x, below]
            t = t + u * pltpu.roll(v, LANES - 1, 1) + pltpu.roll(u * v, 1, 1)
            left = rem[x, mid] - (v - t)
            heading = keep * v + add * left
            return [
                (rem, (x, mid), left),
                (new, (x, mid), heading),
                (cor, (x, mid), cor[x, mid] + heading),
            ]

        return body

    old, new = ha, hb
    for turn in range(1, CHEB):
        following = 1.0 / (2.0 * theta / delta - ratio)
        halo = CW - turn
        lo, hi = CX0 - halo, CX0 + CX + halo
        step = coarse_step(
            old, new, CY0 - halo, CY + 2 * halo, following * ratio, 2.0 * following / delta
        )
        planes(lo, hi, step, {20: 5, 18: 6, 16: 4, 14: 7, 12: 6}[hi - lo])
        ratio = following
        old, new = new, old

    spread = lane_map(LANES, 2 * LANES, lambda i, o: o // 2 == i)
    top = CX + 4
    near_recv()
    region = (pl.ds(CX0 - 2, top), pl.ds(CY0 - 2, CY + 8))
    picked = cor[region] * near[region]
    wide[...] = zdot(picked.reshape(top * (CY + 8), LANES), spread)
    p_recv()

    def prolong(c, slot):
        x = 2 * c + X0 - 4
        stores = []
        for h in range(2):
            part_h = wide[pl.ds(pl.multiple_of(c * (CY + 8), 8), CY + 4), pl.ds(h * LANES, LANES)]
            ebuf[slot, h, pl.ds(R0, RN // 2, stride=2)] = part_h
            ebuf[slot, h, pl.ds(R0 + 1, RN // 2, stride=2)] = part_h
            for k in range(2):
                stores.append((pc, (h, x + k, rows), pc[h, x + k, rows] + ebuf[slot, h, rows]))
        return stores

    planes(0, top, prolong, 4)
    planes(X0 - W + 1, X0 + PX + W - 1, sweep(pc, pa), 5)
    p_sent()
    planes(X0 - 1, X0 + PX + 1, sweep(pa, pb), 6)

    def finish(x, _):
        v, r = residual(pb, x)
        stores = []
        for h in range(2):
            at = (x - X0, pl.ds(0, PY), pl.ds(h * LANES, LANES))
            stores += [(out_p, at, v[h]), (out_r, at, r[h])]
        return stores

    planes(X0, X0 + PX, finish, 4)
    ph_sent()
    src_sent()
    cw_sent()
    near_sent()


def write_out(p, r, out_p, out_r, sem):
    copies = [pltpu.make_async_copy(p, out_p, sem.at[0]), pltpu.make_async_copy(r, out_r, sem.at[1])]
    for copy in copies:
        copy.start()
    for copy in copies:
        copy.wait()


def per_device(source, phases):
    ns, ng = lax.axis_size("space"), lax.axis_size("group")
    fine = (2, FX, FY, LANES)
    coarse = (GX, GY, LANES)
    vmem = pltpu.VMEM
    scratch = [vmem(fine, jnp.int32)]
    scratch += [vmem(fine, F32)] * 11
    scratch += [vmem((3,) + coarse, F32), vmem((CX + 1, CS, LANES), F32)]
    scratch += [vmem(coarse, F32)] * 5
    scratch += [
        vmem((5, (CX + 1) * CS, 2 * LANES), F32),
        vmem((4, 2, PY, LANES), F32),
        vmem((4, 2, FY, LANES), F32),
        vmem(((CX + 4) * (CY + 8), 2 * LANES), F32),
        vmem((2, 1, LANES), F32),
        vmem((4 * ng, 1, LANES), F32),
        vmem((ns // 4, 1, LANES), F32),
        pltpu.SemaphoreType.DMA((2, 2)),
        pltpu.SemaphoreType.DMA((2,)),
        pltpu.SemaphoreType.DMA((2,)),
        pltpu.SemaphoreType.DMA((MESSAGES,)),
        pltpu.SemaphoreType.DMA((MESSAGES,)),
    ]
    out_shape = [jax.ShapeDtypeStruct(source.shape, F32)] * 2
    pressure, residual = pl.pallas_call(
        functools.partial(kernel, ns, ng),
        out_shape=out_shape,
        in_specs=[pl.BlockSpec(memory_space=pltpu.HBM)] * 2,
        out_specs=[pl.BlockSpec(memory_space=pltpu.VMEM)] * 2,
        scratch_shapes=scratch,
        compiler_params=pltpu.CompilerParams(
            collective_id=0, has_side_effects=True, vmem_limit_bytes=40 * 2**20
        ),
    )(source, phases)
    return pl.pallas_call(
        write_out,
        out_shape=out_shape,
        in_specs=[pl.BlockSpec(memory_space=pl.ANY)] * 2,
        out_specs=[pl.BlockSpec(memory_space=pl.ANY)] * 2,
        scratch_shapes=[pltpu.SemaphoreType.DMA((2,))],
        compiler_params=pltpu.CompilerParams(vmem_limit_bytes=2**20),
    )(pressure, residual)


def solution(mesh):
    spec = P("space", "group", None)
    return jax.shard_map(
        per_device, mesh=mesh, in_specs=(spec, spec), out_specs=(spec, spec), check_vma=False
    )
```

```python
import functools
import math

import jax
import jax.numpy as jnp
from jax import lax
from jax.experimental import pallas as pl
from jax.experimental.pallas import tpu as pltpu
from jax.sharding import PartitionSpec as P

CHEB = 6
PHASES = 8
REACTION = 0.01
RELAX = 0.8
LOWER = 0.05
UPPER = 2.0

F32 = jnp.float32
MESH = pl.DeviceIdType.MESH

PX, PY, LANES = 16, 64, 128
X0, Y0 = 4, 8
FX, FY = PX + 2 * X0, PY + 2 * Y0
W = 3
R0, RN = 4, 72
CX, CY = PX // 2, PY // 2
CW, CX0, CY0 = 5, 5, 8
GX, GY = CX + 2 * CX0, CY + 2 * CY0
CS = CY + 8
DIRS = [(-1, 0), (1, 0), (0, -1), (0, 1), (-1, -1), (-1, 1), (1, -1), (1, 1)]
MESSAGES = 8 * 4 + 16 + 12
NO_CELL = 1 << 20
NEAR, NEAR_ROWS, FAR_ROWS = 2, 4, 2


def spans(step, start, size, near, far):
    if step == 0:
        return pl.ds(start, size), pl.ds(start, size)
    width = far - near
    if step > 0:
        return pl.ds(start + size - far, width), pl.ds(start - far, width)
    return pl.ds(start + near, width), pl.ds(start + size + near, width)


def harmonic(left, right):
    return 2.0 * left * right / jnp.maximum(left + right, 1e-30)


def zdot(x, matrix):
    high = x.astype(jnp.bfloat16)
    rest = x - high.astype(F32)
    mid = rest.astype(jnp.bfloat16)
    low = (rest - mid.astype(F32)).astype(jnp.bfloat16)
    dot = functools.partial(jnp.dot, preferred_element_type=F32)
    return dot(high, matrix) + dot(mid, matrix) + dot(low, matrix)


def lane_map(rows, cols, place):
    i = lax.broadcasted_iota(jnp.int32, (rows, cols), 0)
    o = lax.broadcasted_iota(jnp.int32, (rows, cols), 1)
    return jnp.where(place(i, o), 1.0, 0.0).astype(jnp.bfloat16)


def planes(lo, hi, body, k=1):
    def run(first, count):
        stores = [store for j in range(count) for store in body(first + j, j)]
        for ref, at, value in stores:
            ref[at] = value

    def step(j, carry):
        run(lo + j * k, k)
        return carry

    whole = (hi - lo) // k
    lax.fori_loop(0, whole, step, 0)
    if (hi - lo) % k:
        run(lo + whole * k, (hi - lo) % k)


def kernel(
    ns, ng, source_hbm, phases_hbm, out_p, out_r,
    ph, src, kap, wx, wy, wz, dg, di, fo, pa, pb, pc,
    cw, cc, rem, ha, hb, cor, near, zbuf, ybuf, ebuf,
    part, sum1, sum2,
    in_sem, psend, precv, send, recv,
):
    s, g = lax.axis_index("space"), lax.axis_index("group")
    lane = lax.broadcasted_iota(jnp.int32, (1, LANES), 1)
    first, last = lane == 0, lane == LANES - 1

    def here(dx, dy):
        ok = jnp.bool_(True)
        if dx < 0:
            ok = s > 0
        if dx > 0:
            ok = s < ns - 1
        if dy < 0:
            ok = jnp.logical_and(ok, g > 0)
        if dy > 0:
            ok = jnp.logical_and(ok, g < ng - 1)
        return ok

    def halves(hbm, ref, sem):
        return [
            pltpu.make_async_copy(
                hbm.at[:, :, pl.ds(h * LANES, LANES)],
                ref.at[h, pl.ds(X0, PX), pl.ds(Y0, PY)],
                sem.at[h],
            )
            for h in range(2)
        ]

    load_ph = halves(phases_hbm, ph, in_sem.at[0])
    load_src = halves(source_hbm, src, in_sem.at[1])
    for copy in load_ph + load_src:
        copy.start()

    x4, q = lax.rem(s, 4), s // 4
    nq = ns // 4
    n1 = 4 * ng
    me1 = x4 * ng + g

    def peer1(j):
        t = lax.rem(me1 + j, n1)
        return (q * 4 + t // ng, lax.rem(t, ng))

    def peer2(j):
        return (lax.rem(q + j, nq) * 4 + x4, g)

    barrier = pltpu.get_barrier_semaphore()
    expected = jnp.int32(n1 - 1 + nq - 1)

    def greet(peer):
        pl.semaphore_signal(barrier, inc=1, device_id=peer, device_id_type=MESH)

    for j in range(1, n1):
        greet(peer1(j))
    for j in range(1, nq):
        greet(peer2(j))
    for dx, dy in DIRS:
        ok = here(dx, dy)

        @pl.when(ok)
        def _():
            greet((s + dx, g + dy))

        expected = expected + ok.astype(jnp.int32)

    used = [0]

    def exchange(messages):
        base = used[0]
        used[0] += len(messages)

        def copy(k):
            (dx, dy), source, target = messages[k]
            return pltpu.make_async_remote_copy(
                src_ref=source,
                dst_ref=target,
                send_sem=send.at[base + k],
                recv_sem=recv.at[base + k],
                device_id=(s + dx, g + dy),
                device_id_type=MESH,
            )

        def each(sign, act):
            for k, ((dx, dy), _, _) in enumerate(messages):

                @pl.when(here(sign * dx, sign * dy))
                def _():
                    act(copy(k))

        return (
            lambda: each(1, lambda c: c.start()),
            lambda: each(-1, lambda c: c.wait_recv()),
            lambda: each(1, lambda c: c.wait_send()),
        )

    def fill(messages, value):
        for (dx, dy), _, target in messages:

            @pl.when(jnp.logical_not(here(-dx, -dy)))
            def _():
                target[...] = jnp.full(target.shape, value, target.dtype)

    def fine_messages(a, b, width, skip=0):
        messages = []
        for dx, dy in DIRS:
            reach = width - 1 if dx and dy else width
            sx, tx = spans(dx, X0, PX, 0 if dy else skip, reach)
            sy, ty = spans(dy, Y0, PY, 0, reach)
            messages.append(((dx, dy), a.at[:, sx, sy], b.at[:, tx, ty]))
        return messages

    def coarse_messages(a, parts):
        messages = []
        for dx, dy in DIRS:
            if dx and dy:
                boxes = [(0, NEAR, NEAR_ROWS, None), (NEAR, CW - 1, FAR_ROWS, None)]
            else:
                boxes = [(0, far, CW, span) for span, far in parts or [(None, CW)]]
            for after, far, count, span in boxes:
                sx, tx = spans(dx, CX0, CX, after, far)
                sy, ty = spans(dy, CY0, CY, 0, count)
                lead = () if parts is None else (span or slice(None),)
                messages.append(((dx, dy), a.at[lead + (sx, sy)], a.at[lead + (tx, ty)]))
        return messages

    ph_all = fine_messages(ph, ph, W)
    src_all = fine_messages(src, src, W - 1)
    p_all = fine_messages(pb, pc, W, 1)
    cw_all = coarse_messages(cw, [(pl.ds(0, 1), CW), (pl.ds(1, 2), CW - 1)])
    rem_all = coarse_messages(rem, None)
    near_all = []
    for dx, dy in DIRS:
        reach = 1 if dx and dy else 2
        sx, tx = spans(dx, CX0, CX, 0, reach)
        sy, ty = spans(dy, CY0, CY, 0, reach)
        near_all.append(((dx, dy), near.at[sx, sy], near.at[tx, ty]))
    fill(fine_messages(ph, ph, W), NO_CELL)
    for messages in (src_all, p_all, cw_all, rem_all, near_all):
        fill(messages, 0)
    ph_start, ph_recv, ph_sent = exchange(ph_all)
    src_start, src_recv, src_sent = exchange(src_all)
    cw_start, cw_recv, cw_sent = exchange(cw_all)
    rem_start, rem_recv, rem_sent = exchange(rem_all)
    p_start, p_recv, p_sent = exchange(p_all)
    near_start, near_recv, near_sent = exchange(near_all)

    def conductivity(x, r0, n):
        at = pl.ds(r0, n)
        rate = -6.0 * math.log(10.0) / (PHASES - 1)
        return [(kap, (h, x, at), jnp.exp(ph[h, x, at].astype(F32) * rate)) for h in range(2)]

    def faces(x, r0, n):
        rows, above = pl.ds(r0, n), pl.ds(r0 + 1, n)
        k = [kap[h, x, rows] for h in range(2)]
        up = [pltpu.roll(k[h], LANES - 1, 1) for h in range(2)]
        beside = [jnp.where(last, up[1], up[0]), jnp.where(last, 0.0, up[1])]
        stores = []
        for h in range(2):
            stores.append((wx, (h, x, rows), harmonic(k[h], kap[h, x + 1, rows])))
            stores.append((wy, (h, x, rows), harmonic(k[h], kap[h, x, above])))
            stores.append((wz, (h, x, rows), harmonic(k[h], beside[h])))
        return stores

    def diagonal(x, r0, n):
        rows, below = pl.ds(r0, n), pl.ds(r0 - 1, n)
        z = [wz[h, x, rows] for h in range(2)]
        down = [pltpu.roll(z[h], 1, 1) for h in range(2)]
        beside = [jnp.where(first, 0.0, down[0]), jnp.where(first, down[0], down[1])]
        stores = []
        for h in range(2):
            d = REACTION * kap[h, x, rows] + wx[h, x, rows] + wx[h, x - 1, rows]
            d = d + wy[h, x, rows] + wy[h, x, below] + z[h] + beside[h]
            stores.append((dg, (h, x, rows), d))
            scaled = jnp.where(d > 0.0, RELAX / jnp.where(d > 0.0, d, 1.0), 0.0)
            stores.append((di, (h, x, rows), scaled))
        return stores

    for copy in load_ph:
        copy.wait()
    planes(X0, X0 + PX, lambda x, _: conductivity(x, Y0, PY), 4)

    for copy in load_src:
        copy.wait()

    def add_plane(x, total):
        plane = src[0, x, pl.ds(Y0, PY)] + src[1, x, pl.ds(Y0, PY)]
        return total + jnp.sum(plane.reshape(PY // 8, 8, LANES), axis=0)

    local = lax.fori_loop(X0, X0 + PX, add_plane, jnp.zeros((8, LANES), F32))
    local = jnp.sum(local, axis=0, keepdims=True)
    part[0] = local
    sum1[me1] = local

    pl.semaphore_wait(barrier, expected)

    def gather_part(stage, slots, count, me, peer):
        def start():
            for j in range(1, count):
                pltpu.make_async_remote_copy(
                    src_ref=part.at[stage],
                    dst_ref=slots.at[me],
                    send_sem=psend.at[stage],
                    recv_sem=precv.at[stage],
                    device_id=peer(j),
                    device_id_type=MESH,
                ).start()

        def wait():
            pltpu.make_async_remote_copy(
                src_ref=slots.at[pl.ds(0, count - 1)],
                dst_ref=slots.at[pl.ds(0, count - 1)],
                send_sem=psend.at[stage],
                recv_sem=precv.at[stage],
                device_id=peer(1),
                device_id_type=MESH,
            ).wait()

        return start, wait

    start1, wait1 = gather_part(0, sum1, n1, me1, peer1)
    start2, wait2 = gather_part(1, sum2, nq, q, peer2)
    start1()
    ph_start()
    src_start()

    planes(X0, X0 + PX, lambda x, _: faces(x, Y0, PY), 4)

    wait1()
    total1 = jnp.sum(sum1[...], axis=0)
    part[1] = total1
    sum2[q] = total1
    start2()

    planes(X0 + 1, X0 + PX - 1, lambda x, _: diagonal(x, Y0, PY), 7)

    ph_recv()

    def sides(body, lo, hi):
        def both_sides(x, _):
            return body(x, lo, 8) + body(x, hi, 8)

        return both_sides

    planes(X0, X0 + PX, sides(conductivity, 0, FY - 8), 4)
    for lo in (X0 - W, X0 + PX):
        planes(lo, lo + W, lambda x, _: conductivity(x, 0, FY), 3)
    for lo, hi in ((X0 - W, X0 + 1), (X0 + PX - 1, X0 + PX + W - 1)):
        planes(lo, hi, lambda x, _: faces(x, R0, RN), 2)
    planes(X0 + 1, X0 + PX - 1, sides(faces, R0, R0 + RN - 8), 7)

    both = lane_map(2 * LANES, LANES, lambda i, o: i // 2 == o)
    upper = lane_map(2 * LANES, LANES, lambda i, o: i == 2 * o + 1)
    outer = lane_map(2 * LANES, LANES, lambda i, o: (i == 2 * o + 1) | (i == 2 * o - 1))
    even, odd = pl.ds(Y0, CY + 1, stride=2), pl.ds(Y0 + 1, CY + 1, stride=2)
    under = pl.ds(Y0 - 1, CY + 1, stride=2)

    def pair(ref, h, x):
        return ref[h, x, even] + ref[h, x, odd]

    def coarse_parts(i, _):
        a = X0 + 2 * i
        b = a + 1
        rows = pl.ds(pl.multiple_of(i * CS, 8), CY + 1)
        stores = []
        for h in range(2):
            cols = pl.ds(h * LANES, LANES)
            east = pair(wx, h, b)
            north = wy[h, a, odd] + wy[h, b, odd]
            south = wy[h, a, under] + wy[h, b, under]
            kept = REACTION * (pair(kap, h, a) + pair(kap, h, b))
            middle = kept + east + pair(wx, h, a - 1) + north + south
            for k, value in enumerate((middle, east, north, pair(wz, h, a) + pair(wz, h, b))):
                stores.append((zbuf, (k, rows, cols), value))
        return stores

    planes(0, CX + 1, coarse_parts, 3)

    flat = pl.ds(0, CX * CS)
    center = zdot(zbuf[0], both) + zdot(zbuf[3], outer)
    safe = jnp.where(center > 0.0, center, 1.0)
    d = lax.rsqrt(safe)
    d = jnp.where(center > 0.0, d * (1.5 - 0.5 * safe * d * d), 0.0)
    cc[...] = d.reshape(CX + 1, CS, LANES)
    weights = [zdot(zbuf[k, flat], m) for k, m in ((1, both), (2, both), (3, upper))]
    for k in range(3):
        zbuf[k, flat, pl.ds(0, LANES)] = weights[k]

    def scale(i, _):
        x = CX0 + i
        at, to = pl.ds(0, CY), pl.ds(CY0, CY)
        src_rows = pl.ds(pl.multiple_of(i * CS, 8), CY)
        mine = cc[i, at]
        beside = (cc[i + 1, at], cc[i, pl.ds(1, CY)], pltpu.roll(mine, LANES - 1, 1))
        stores = []
        for k in range(3):
            value = zbuf[k, src_rows, pl.ds(0, LANES)] * mine * beside[k]
            stores.append((cw, (k, x, to), value))
        return stores

    planes(0, CX, scale, 4)

    cw_start()

    for lo, hi in ((X0 - W + 1, X0 + 1), (X0 + PX - 1, X0 + PX + W - 1)):
        planes(lo, hi, lambda x, _: diagonal(x, R0, RN), 3)
    planes(X0 + 1, X0 + PX - 1, sides(diagonal, R0, R0 + RN - 8), 7)

    wait2()
    total = jnp.sum(sum2[...], axis=0)
    average = jnp.sum(total, axis=1, keepdims=True) * (1.0 / (PX * ns * PY * ng * 2 * LANES))
    src_recv()

    rows = pl.ds(R0, RN)

    def first_sweep(x, _):
        stores = []
        for h in range(2):
            f = kap[h, x, rows] * (src[h, x, rows] - average)
            stores.append((fo, (h, x, rows), f))
            stores.append((pa, (h, x, rows), di[h, x, rows] * f))
        return stores

    planes(X0 - W + 1, X0 + PX + W - 1, first_sweep, 4)

    def beside_sum(p, x, r0, n):
        mid, above, below = pl.ds(r0, n), pl.ds(r0 + 1, n), pl.ds(r0 - 1, n)
        v = [p[h, x, mid] for h in range(2)]
        z = [wz[h, x, mid] for h in range(2)]
        up = [pltpu.roll(v[h], LANES - 1, 1) for h in range(2)]
        down = [pltpu.roll(z[h] * v[h], 1, 1) for h in range(2)]
        up[0] = jnp.where(last, up[1], up[0])
        down = [jnp.where(first, 0.0, down[0]), jnp.where(first, down[0], down[1])]
        sums = []
        for h in range(2):
            t = wx[h, x, mid] * p[h, x + 1, mid] + wx[h, x - 1, mid] * p[h, x - 1, mid]
            t = t + wy[h, x, mid] * p[h, x, above] + wy[h, x, below] * p[h, x, below]
            sums.append(t + z[h] * up[h] + down[h])
        return v, sums

    def sweep(old, new, *strips):
        def body(x, _):
            stores = []
            for r0, n in strips or ((R0, RN),):
                at = pl.ds(r0, n)
                v, t = beside_sum(old, x, r0, n)
                for h in range(2):
                    value = (1.0 - RELAX) * v[h] + di[h, x, at] * (fo[h, x, at] + t[h])
                    stores.append((new, (h, x, at), value))
            return stores

        return body

    mid = pl.ds(Y0, PY)

    def residual(p, x):
        v, t = beside_sum(p, x, Y0, PY)
        return v, [fo[h, x, mid] - dg[h, x, mid] * v[h] + t[h] for h in range(2)]

    planes(X0 - 1, X0 + PX + 1, sweep(pa, pb), 6)

    def restrict(i, slot):
        a = X0 + 2 * i
        va, ra = residual(pb, a)
        vb, rb = residual(pb, a + 1)
        dst = pl.ds(pl.multiple_of(i * CY, CY), CY)
        stores = []
        for h in range(2):
            stores.append((pc, (h, a, mid), va[h]))
            stores.append((pc, (h, a + 1, mid), vb[h]))
            ybuf[slot, h] = ra[h] + rb[h]
            halves_y = ybuf[slot, h, pl.ds(0, CY, stride=2)] + ybuf[slot, h, pl.ds(1, CY, stride=2)]
            stores.append((zbuf, (4, dst, pl.ds(h * LANES, LANES)), halves_y))
        return stores

    planes(0, CX, restrict, 4)
    coarse_forcing = zdot(zbuf[4, pl.ds(0, CX * CY)], both).reshape(CX, CY, LANES)
    rem[pl.ds(CX0, CX), pl.ds(CY0, CY)] = coarse_forcing * cc[pl.ds(0, CX), pl.ds(0, CY)]
    rem_start()
    for x in (X0 - 1, X0 + PX):
        pc[:, x, mid] = pb[:, x, mid]

    theta = (UPPER + LOWER) / 2.0
    delta = (UPPER - LOWER) / 2.0
    ratio = delta / theta
    body_rows = pl.ds(CY0 - CW, CY + 2 * CW)
    cw_recv()
    p_start()
    rem_recv()
    rem_sent()

    def first_heading(x, _):
        heading = rem[x, body_rows] * (1.0 / theta)
        return [(ha, (x, body_rows), heading), (cor, (x, body_rows), heading)]

    planes(0, GX, first_heading, 6)

    def coarse_step(old, new, r0, n, keep, add):
        mid, above, below = pl.ds(r0, n), pl.ds(r0 + 1, n), pl.ds(r0 - 1, n)

        def body(x, _):
            v = old[x, mid]
            u = cw[2, x, mid]
            t = cw[0, x, mid] * old[x + 1, mid] + cw[0, x - 1, mid] * old[x - 1, mid]
            t = t + cw[1, x, mid] * old[x, above] + cw[1, x, below] * old[x, below]
            t = t + u * pltpu.roll(v, LANES - 1, 1) + pltpu.roll(u * v, 1, 1)
            left = rem[x, mid] - (v - t)
            heading = keep * v + add * left
            return [
                (rem, (x, mid), left),
                (new, (x, mid), heading),
                (cor, (x, mid), cor[x, mid] + heading),
            ]

        return body

    old, new = ha, hb
    for turn in range(1, CHEB):
        following = 1.0 / (2.0 * theta / delta - ratio)
        halo = CW - turn
        lo, hi = CX0 - halo, CX0 + CX + halo
        step = coarse_step(
            old, new, CY0 - halo, CY + 2 * halo, following * ratio, 2.0 * following / delta
        )
        planes(lo, hi, step, {16: 4, 14: 7, 12: 6, 10: 5, 8: 4}[hi - lo])
        ratio = following
        old, new = new, old

    inside = (pl.ds(CX0, CX), pl.ds(CY0, CY))
    near[inside] = cor[inside] * cc[pl.ds(0, CX), pl.ds(0, CY)]
    near_start()
    spread = lane_map(LANES, 2 * LANES, lambda i, o: o // 2 == i)

    def prolong(part, c, r, n, slot):
        x, r0 = X0 + 2 * (c - CX0), Y0 + 2 * (r - CY0)
        at = pl.ds(r0, 2 * n)
        stores = []
        for h in range(2):
            value = part[:, h * LANES : (h + 1) * LANES]
            ebuf[slot, h, pl.ds(r0, n, stride=2)] = value
            ebuf[slot, h, pl.ds(r0 + 1, n, stride=2)] = value
            for k in range(2):
                stores.append((pc, (h, x + k, at), pc[h, x + k, at] + ebuf[slot, h, at]))
        return stores

    zbuf[0, pl.ds(0, CX * CY)] = zdot(near[inside].reshape(CX * CY, LANES), spread)

    def prolong_inside(i, slot):
        part = zbuf[0, pl.ds(pl.multiple_of(i * CY, CY), CY)]
        return prolong(part, CX0 + i, CY0, CY, slot)

    planes(0, CX, prolong_inside, 4)
    edge = 12
    planes(X0 + 1, X0 + PX - 1, sweep(pc, pa, (R0 + edge, RN - 2 * edge)), 7)

    p_recv()
    near_recv()
    tall = CY + 8
    sides_x = (CX0 - 2, CX0 - 1, CX0 + CX, CX0 + CX + 1)
    for k, c in enumerate(sides_x):
        zbuf[1, pl.ds(k * tall, tall)] = zdot(near[c, pl.ds(CY0 - 2, tall)], spread)
    for k, r in enumerate((CY0 - 8, CY0 + CY)):
        strip = near[pl.ds(CX0, CX), pl.ds(r, 8)].reshape(CX * 8, LANES)
        zbuf[2, pl.ds(k * CX * 8, CX * 8)] = zdot(strip, spread)
    for k, c in enumerate(sides_x):
        part = zbuf[1, pl.ds(k * tall, CY + 4)]
        for ref, at, value in prolong(part, c, CY0 - 2, CY + 4, k):
            ref[at] = value

    for i in range(CX):
        low = zbuf[2, pl.ds(i * 8 + 6, 2)]
        high = zbuf[2, pl.ds(CX * 8 + i * 8, 2)]
        stores = prolong(low, CX0 + i, CY0 - 2, 2, i % 4)
        for ref, at, value in stores + prolong(high, CX0 + i, CY0 + CY, 2, i % 4):
            ref[at] = value
    for lo, hi in ((X0 - W + 1, X0 + 1), (X0 + PX - 1, X0 + PX + W - 1)):
        planes(lo, hi, sweep(pc, pa), 3)
    planes(X0 + 1, X0 + PX - 1, sweep(pc, pa, (R0, edge), (R0 + RN - edge, edge)), 7)
    p_sent()
    planes(X0 - 1, X0 + PX + 1, sweep(pa, pb), 6)

    def finish(x, _):
        v, r = residual(pb, x)
        stores = []
        for h in range(2):
            at = (x - X0, pl.ds(0, PY), pl.ds(h * LANES, LANES))
            stores += [(out_p, at, v[h]), (out_r, at, r[h])]
        return stores

    planes(X0, X0 + PX, finish, 4)
    ph_sent()
    src_sent()
    cw_sent()
    near_sent()


def write_out(p, r, out_p, out_r, sem):
    copies = [pltpu.make_async_copy(p, out_p, sem.at[0]), pltpu.make_async_copy(r, out_r, sem.at[1])]
    for copy in copies:
        copy.start()
    for copy in copies:
        copy.wait()


def per_device(source, phases):
    ns, ng = lax.axis_size("space"), lax.axis_size("group")
    fine = (2, FX, FY, LANES)
    coarse = (GX, GY, LANES)
    vmem = pltpu.VMEM
    scratch = [vmem(fine, jnp.int32)]
    scratch += [vmem(fine, F32)] * 11
    scratch += [vmem((3,) + coarse, F32), vmem((CX + 1, CS, LANES), F32)]
    scratch += [vmem(coarse, F32)] * 5
    scratch += [
        vmem((5, (CX + 1) * CS, 2 * LANES), F32),
        vmem((4, 2, PY, LANES), F32),
        vmem((4, 2, FY, LANES), F32),
        vmem((2, 1, LANES), F32),
        vmem((4 * ng, 1, LANES), F32),
        vmem((ns // 4, 1, LANES), F32),
        pltpu.SemaphoreType.DMA((2, 2)),
        pltpu.SemaphoreType.DMA((2,)),
        pltpu.SemaphoreType.DMA((2,)),
        pltpu.SemaphoreType.DMA((MESSAGES,)),
        pltpu.SemaphoreType.DMA((MESSAGES,)),
    ]
    out_shape = [jax.ShapeDtypeStruct(source.shape, F32)] * 2
    pressure, residual = pl.pallas_call(
        functools.partial(kernel, ns, ng),
        out_shape=out_shape,
        in_specs=[pl.BlockSpec(memory_space=pltpu.HBM)] * 2,
        out_specs=[pl.BlockSpec(memory_space=pltpu.VMEM)] * 2,
        scratch_shapes=scratch,
        compiler_params=pltpu.CompilerParams(
            collective_id=0, has_side_effects=True, vmem_limit_bytes=40 * 2**20
        ),
    )(source, phases)
    return pl.pallas_call(
        write_out,
        out_shape=out_shape,
        in_specs=[pl.BlockSpec(memory_space=pl.ANY)] * 2,
        out_specs=[pl.BlockSpec(memory_space=pl.ANY)] * 2,
        scratch_shapes=[pltpu.SemaphoreType.DMA((2,))],
        compiler_params=pltpu.CompilerParams(vmem_limit_bytes=2**20),
    )(pressure, residual)


def solution(mesh):
    spec = P("space", "group", None)
    return jax.shard_map(
        per_device, mesh=mesh, in_specs=(spec, spec), out_specs=(spec, spec), check_vma=False
    )
```

```python
import functools
import math

import jax
import jax.numpy as jnp
from jax import lax
from jax.experimental import pallas as pl
from jax.experimental.pallas import tpu as pltpu
from jax.sharding import PartitionSpec as P

CHEB = 6
PHASES = 8
REACTION = 0.01
RELAX = 0.8
LOWER = 0.05
UPPER = 2.0

F32 = jnp.float32
MESH = pl.DeviceIdType.MESH

PX, PY, LANES = 16, 64, 128
X0, Y0 = 4, 8
FX, FY = PX + 2 * X0, PY + 2 * Y0
W = 3
R0, RN = 4, 72
CX, CY = PX // 2, PY // 2
CW, CX0, CY0 = 5, 5, 8
GX, GY = CX + 2 * CX0, CY + 2 * CY0
CS = CY + 8
DIRS = [(-1, 0), (1, 0), (0, -1), (0, 1), (-1, -1), (-1, 1), (1, -1), (1, 1)]
MESSAGES = 8 * 4 + 16 + 12
NO_CELL = 1 << 20
NEAR, NEAR_ROWS, FAR_ROWS = 2, 4, 2


def spans(step, start, size, near, far):
    if step == 0:
        return pl.ds(start, size), pl.ds(start, size)
    width = far - near
    if step > 0:
        return pl.ds(start + size - far, width), pl.ds(start - far, width)
    return pl.ds(start + near, width), pl.ds(start + size + near, width)


def harmonic(left, right):
    return 2.0 * left * right / jnp.maximum(left + right, 1e-30)


def zdot(x, matrix):
    high = x.astype(jnp.bfloat16)
    rest = x - high.astype(F32)
    mid = rest.astype(jnp.bfloat16)
    low = (rest - mid.astype(F32)).astype(jnp.bfloat16)
    dot = functools.partial(jnp.dot, preferred_element_type=F32)
    return dot(high, matrix) + dot(mid, matrix) + dot(low, matrix)


def lane_map(rows, cols, place):
    i = lax.broadcasted_iota(jnp.int32, (rows, cols), 0)
    o = lax.broadcasted_iota(jnp.int32, (rows, cols), 1)
    return jnp.where(place(i, o), 1.0, 0.0).astype(jnp.bfloat16)


def planes(lo, hi, body, k=1):
    def run(first, count):
        stores = [store for j in range(count) for store in body(first + j, j)]
        for ref, at, value in stores:
            ref[at] = value

    def step(j, carry):
        run(lo + j * k, k)
        return carry

    whole = (hi - lo) // k
    lax.fori_loop(0, whole, step, 0)
    if (hi - lo) % k:
        run(lo + whole * k, (hi - lo) % k)


def beside_sum(p, weights, x, r0, n):
    wx, wy, wz = weights
    lane = lax.broadcasted_iota(jnp.int32, (1, LANES), 1)
    first, last = lane == 0, lane == LANES - 1
    mid, above, below = pl.ds(r0, n), pl.ds(r0 + 1, n), pl.ds(r0 - 1, n)
    v = [p[h, x, mid] for h in range(2)]
    z = [wz[h, x, mid] for h in range(2)]
    up = [pltpu.roll(v[h], LANES - 1, 1) for h in range(2)]
    down = [pltpu.roll(z[h] * v[h], 1, 1) for h in range(2)]
    up[0] = jnp.where(last, up[1], up[0])
    down = [jnp.where(first, 0.0, down[0]), jnp.where(first, down[0], down[1])]
    sums = []
    for h in range(2):
        t = wx[h, x, mid] * p[h, x + 1, mid] + wx[h, x - 1, mid] * p[h, x - 1, mid]
        t = t + wy[h, x, mid] * p[h, x, above] + wy[h, x, below] * p[h, x, below]
        sums.append(t + z[h] * up[h] + down[h])
    return v, sums


def residual(p, weights, fo, dg, x):
    mid = pl.ds(Y0, PY)
    v, t = beside_sum(p, weights, x, Y0, PY)
    return v, [fo[h, x, mid] - dg[h, x, mid] * v[h] + t[h] for h in range(2)]


def kernel(
    ns, ng, source_hbm, phases_hbm, wx, wy, wz, dg, fo, pb,
    ph, src, kap, di, pa, pc,
    cw, cc, rem, ha, hb, cor, near, zbuf, ybuf, ebuf,
    part, sum1, sum2,
    in_sem, psend, precv, send, recv,
):
    s, g = lax.axis_index("space"), lax.axis_index("group")
    lane = lax.broadcasted_iota(jnp.int32, (1, LANES), 1)
    first, last = lane == 0, lane == LANES - 1

    def here(dx, dy):
        ok = jnp.bool_(True)
        if dx < 0:
            ok = s > 0
        if dx > 0:
            ok = s < ns - 1
        if dy < 0:
            ok = jnp.logical_and(ok, g > 0)
        if dy > 0:
            ok = jnp.logical_and(ok, g < ng - 1)
        return ok

    def halves(hbm, ref, sem):
        return [
            pltpu.make_async_copy(
                hbm.at[:, :, pl.ds(h * LANES, LANES)],
                ref.at[h, pl.ds(X0, PX), pl.ds(Y0, PY)],
                sem.at[h],
            )
            for h in range(2)
        ]

    load_ph = halves(phases_hbm, ph, in_sem.at[0])
    load_src = halves(source_hbm, src, in_sem.at[1])
    for copy in load_ph + load_src:
        copy.start()

    x4, q = lax.rem(s, 4), s // 4
    nq = ns // 4
    n1 = 4 * ng
    me1 = x4 * ng + g

    def peer1(j):
        t = lax.rem(me1 + j, n1)
        return (q * 4 + t // ng, lax.rem(t, ng))

    def peer2(j):
        return (lax.rem(q + j, nq) * 4 + x4, g)

    barrier = pltpu.get_barrier_semaphore()
    expected = jnp.int32(n1 - 1 + nq - 1)

    def greet(peer):
        pl.semaphore_signal(barrier, inc=1, device_id=peer, device_id_type=MESH)

    for j in range(1, n1):
        greet(peer1(j))
    for j in range(1, nq):
        greet(peer2(j))
    for dx, dy in DIRS:
        ok = here(dx, dy)

        @pl.when(ok)
        def _():
            greet((s + dx, g + dy))

        expected = expected + ok.astype(jnp.int32)

    used = [0]

    def exchange(messages):
        base = used[0]
        used[0] += len(messages)

        def copy(k):
            (dx, dy), source, target = messages[k]
            return pltpu.make_async_remote_copy(
                src_ref=source,
                dst_ref=target,
                send_sem=send.at[base + k],
                recv_sem=recv.at[base + k],
                device_id=(s + dx, g + dy),
                device_id_type=MESH,
            )

        def each(sign, act):
            for k, ((dx, dy), _, _) in enumerate(messages):

                @pl.when(here(sign * dx, sign * dy))
                def _():
                    act(copy(k))

        return (
            lambda: each(1, lambda c: c.start()),
            lambda: each(-1, lambda c: c.wait_recv()),
            lambda: each(1, lambda c: c.wait_send()),
        )

    def fill(messages, value):
        for (dx, dy), _, target in messages:

            @pl.when(jnp.logical_not(here(-dx, -dy)))
            def _():
                target[...] = jnp.full(target.shape, value, target.dtype)

    def fine_messages(a, b, width, skip=0):
        messages = []
        for dx, dy in DIRS:
            reach = width - 1 if dx and dy else width
            sx, tx = spans(dx, X0, PX, 0 if dy else skip, reach)
            sy, ty = spans(dy, Y0, PY, 0, reach)
            messages.append(((dx, dy), a.at[:, sx, sy], b.at[:, tx, ty]))
        return messages

    def coarse_messages(a, parts):
        messages = []
        for dx, dy in DIRS:
            if dx and dy:
                boxes = [(0, NEAR, NEAR_ROWS, None), (NEAR, CW - 1, FAR_ROWS, None)]
            else:
                boxes = [(0, far, CW, span) for span, far in parts or [(None, CW)]]
            for after, far, count, span in boxes:
                sx, tx = spans(dx, CX0, CX, after, far)
                sy, ty = spans(dy, CY0, CY, 0, count)
                lead = () if parts is None else (span or slice(None),)
                messages.append(((dx, dy), a.at[lead + (sx, sy)], a.at[lead + (tx, ty)]))
        return messages

    ph_all = fine_messages(ph, ph, W)
    src_all = fine_messages(src, src, W - 1)
    p_all = fine_messages(pb, pc, W, 1)
    cw_all = coarse_messages(cw, [(pl.ds(0, 1), CW), (pl.ds(1, 2), CW - 1)])
    rem_all = coarse_messages(rem, None)
    near_all = []
    for dx, dy in DIRS:
        reach = 1 if dx and dy else 2
        sx, tx = spans(dx, CX0, CX, 0, reach)
        sy, ty = spans(dy, CY0, CY, 0, reach)
        near_all.append(((dx, dy), near.at[sx, sy], near.at[tx, ty]))
    fill(fine_messages(ph, ph, W), NO_CELL)
    for messages in (src_all, p_all, cw_all, rem_all, near_all):
        fill(messages, 0)
    ph_start, ph_recv, ph_sent = exchange(ph_all)
    src_start, src_recv, src_sent = exchange(src_all)
    cw_start, cw_recv, cw_sent = exchange(cw_all)
    rem_start, rem_recv, rem_sent = exchange(rem_all)
    p_start, p_recv, p_sent = exchange(p_all)
    near_start, near_recv, near_sent = exchange(near_all)

    def conductivity(x, r0, n):
        at = pl.ds(r0, n)
        rate = -6.0 * math.log(10.0) / (PHASES - 1)
        return [(kap, (h, x, at), jnp.exp(ph[h, x, at].astype(F32) * rate)) for h in range(2)]

    def faces(x, r0, n):
        rows, above = pl.ds(r0, n), pl.ds(r0 + 1, n)
        k = [kap[h, x, rows] for h in range(2)]
        up = [pltpu.roll(k[h], LANES - 1, 1) for h in range(2)]
        beside = [jnp.where(last, up[1], up[0]), jnp.where(last, 0.0, up[1])]
        stores = []
        for h in range(2):
            stores.append((wx, (h, x, rows), harmonic(k[h], kap[h, x + 1, rows])))
            stores.append((wy, (h, x, rows), harmonic(k[h], kap[h, x, above])))
            stores.append((wz, (h, x, rows), harmonic(k[h], beside[h])))
        return stores

    def diagonal(x, r0, n):
        rows, below = pl.ds(r0, n), pl.ds(r0 - 1, n)
        z = [wz[h, x, rows] for h in range(2)]
        down = [pltpu.roll(z[h], 1, 1) for h in range(2)]
        beside = [jnp.where(first, 0.0, down[0]), jnp.where(first, down[0], down[1])]
        stores = []
        for h in range(2):
            d = REACTION * kap[h, x, rows] + wx[h, x, rows] + wx[h, x - 1, rows]
            d = d + wy[h, x, rows] + wy[h, x, below] + z[h] + beside[h]
            stores.append((dg, (h, x, rows), d))
            scaled = jnp.where(d > 0.0, RELAX / jnp.where(d > 0.0, d, 1.0), 0.0)
            stores.append((di, (h, x, rows), scaled))
        return stores

    for copy in load_ph:
        copy.wait()
    planes(X0, X0 + PX, lambda x, _: conductivity(x, Y0, PY), 4)

    for copy in load_src:
        copy.wait()

    def add_plane(x, total):
        plane = src[0, x, pl.ds(Y0, PY)] + src[1, x, pl.ds(Y0, PY)]
        return total + jnp.sum(plane.reshape(PY // 8, 8, LANES), axis=0)

    local = lax.fori_loop(X0, X0 + PX, add_plane, jnp.zeros((8, LANES), F32))
    local = jnp.sum(local, axis=0, keepdims=True)
    part[0] = local
    sum1[me1] = local

    pl.semaphore_wait(barrier, expected)

    def gather_part(stage, slots, count, me, peer):
        def start():
            for j in range(1, count):
                pltpu.make_async_remote_copy(
                    src_ref=part.at[stage],
                    dst_ref=slots.at[me],
                    send_sem=psend.at[stage],
                    recv_sem=precv.at[stage],
                    device_id=peer(j),
                    device_id_type=MESH,
                ).start()

        def wait():
            pltpu.make_async_remote_copy(
                src_ref=slots.at[pl.ds(0, count - 1)],
                dst_ref=slots.at[pl.ds(0, count - 1)],
                send_sem=psend.at[stage],
                recv_sem=precv.at[stage],
                device_id=peer(1),
                device_id_type=MESH,
            ).wait()

        return start, wait

    start1, wait1 = gather_part(0, sum1, n1, me1, peer1)
    start2, wait2 = gather_part(1, sum2, nq, q, peer2)
    start1()
    ph_start()

    planes(X0, X0 + PX, lambda x, _: faces(x, Y0, PY), 4)

    wait1()
    total1 = jnp.sum(sum1[...], axis=0)
    part[1] = total1
    sum2[q] = total1
    start2()
    src_start()

    planes(X0 + 1, X0 + PX - 1, lambda x, _: diagonal(x, Y0, PY), 7)

    ph_recv()

    def sides(body, lo, hi):
        def both_sides(x, _):
            return body(x, lo, 8) + body(x, hi, 8)

        return both_sides

    planes(X0, X0 + PX, sides(conductivity, 0, FY - 8), 4)
    for lo in (X0 - W, X0 + PX):
        planes(lo, lo + W, lambda x, _: conductivity(x, 0, FY), 3)
    for lo, hi in ((X0 - W, X0 + 1), (X0 + PX - 1, X0 + PX + W - 1)):
        planes(lo, hi, lambda x, _: faces(x, R0, RN), 2)
    planes(X0 + 1, X0 + PX - 1, sides(faces, R0, R0 + RN - 8), 7)

    both = lane_map(2 * LANES, LANES, lambda i, o: i // 2 == o)
    upper = lane_map(2 * LANES, LANES, lambda i, o: i == 2 * o + 1)
    outer = lane_map(2 * LANES, LANES, lambda i, o: (i == 2 * o + 1) | (i == 2 * o - 1))
    even, odd = pl.ds(Y0, CY + 1, stride=2), pl.ds(Y0 + 1, CY + 1, stride=2)
    under = pl.ds(Y0 - 1, CY + 1, stride=2)

    def pair(ref, h, x):
        return ref[h, x, even] + ref[h, x, odd]

    def coarse_parts(i, _):
        a = X0 + 2 * i
        b = a + 1
        rows = pl.ds(pl.multiple_of(i * CS, 8), CY + 1)
        stores = []
        for h in range(2):
            cols = pl.ds(h * LANES, LANES)
            east = pair(wx, h, b)
            north = wy[h, a, odd] + wy[h, b, odd]
            south = wy[h, a, under] + wy[h, b, under]
            kept = REACTION * (pair(kap, h, a) + pair(kap, h, b))
            middle = kept + east + pair(wx, h, a - 1) + north + south
            for k, value in enumerate((middle, east, north, pair(wz, h, a) + pair(wz, h, b))):
                stores.append((zbuf, (k, rows, cols), value))
        return stores

    planes(0, CX + 1, coarse_parts, 3)

    flat = pl.ds(0, CX * CS)
    center = zdot(zbuf[0], both) + zdot(zbuf[3], outer)
    safe = jnp.where(center > 0.0, center, 1.0)
    d = lax.rsqrt(safe)
    d = jnp.where(center > 0.0, d * (1.5 - 0.5 * safe * d * d), 0.0)
    cc[...] = d.reshape(CX + 1, CS, LANES)
    weights = [zdot(zbuf[k, flat], m) for k, m in ((1, both), (2, both), (3, upper))]
    for k in range(3):
        zbuf[k, flat, pl.ds(0, LANES)] = weights[k]

    def scale(i, _):
        x = CX0 + i
        at, to = pl.ds(0, CY), pl.ds(CY0, CY)
        src_rows = pl.ds(pl.multiple_of(i * CS, 8), CY)
        mine = cc[i, at]
        beside = (cc[i + 1, at], cc[i, pl.ds(1, CY)], pltpu.roll(mine, LANES - 1, 1))
        stores = []
        for k in range(3):
            value = zbuf[k, src_rows, pl.ds(0, LANES)] * mine * beside[k]
            stores.append((cw, (k, x, to), value))
        return stores

    planes(0, CX, scale, 4)

    cw_start()

    for lo, hi in ((X0 - W + 1, X0 + 1), (X0 + PX - 1, X0 + PX + W - 1)):
        planes(lo, hi, lambda x, _: diagonal(x, R0, RN), 3)
    planes(X0 + 1, X0 + PX - 1, sides(diagonal, R0, R0 + RN - 8), 7)

    wait2()
    total = jnp.sum(sum2[...], axis=0)
    average = jnp.sum(total, axis=1, keepdims=True) * (1.0 / (PX * ns * PY * ng * 2 * LANES))
    src_recv()

    rows = pl.ds(R0, RN)

    def first_sweep(x, _):
        stores = []
        for h in range(2):
            f = kap[h, x, rows] * (src[h, x, rows] - average)
            stores.append((fo, (h, x, rows), f))
            stores.append((pa, (h, x, rows), di[h, x, rows] * f))
        return stores

    planes(X0 - W + 1, X0 + PX + W - 1, first_sweep, 4)

    def sweep(old, new, *strips):
        def body(x, _):
            stores = []
            for r0, n in strips or ((R0, RN),):
                at = pl.ds(r0, n)
                v, t = beside_sum(old, (wx, wy, wz), x, r0, n)
                for h in range(2):
                    value = (1.0 - RELAX) * v[h] + di[h, x, at] * (fo[h, x, at] + t[h])
                    stores.append((new, (h, x, at), value))
            return stores

        return body

    mid = pl.ds(Y0, PY)

    planes(X0 - 1, X0 + PX + 1, sweep(pa, pb), 6)

    def restrict(i, slot):
        a = X0 + 2 * i
        va, ra = residual(pb, (wx, wy, wz), fo, dg, a)
        vb, rb = residual(pb, (wx, wy, wz), fo, dg, a + 1)
        dst = pl.ds(pl.multiple_of(i * CY, CY), CY)
        stores = []
        for h in range(2):
            stores.append((pc, (h, a, mid), va[h]))
            stores.append((pc, (h, a + 1, mid), vb[h]))
            ybuf[slot, h] = ra[h] + rb[h]
            halves_y = ybuf[slot, h, pl.ds(0, CY, stride=2)] + ybuf[slot, h, pl.ds(1, CY, stride=2)]
            stores.append((zbuf, (4, dst, pl.ds(h * LANES, LANES)), halves_y))
        return stores

    planes(0, CX, restrict, 4)
    coarse_forcing = zdot(zbuf[4, pl.ds(0, CX * CY)], both).reshape(CX, CY, LANES)
    rem[pl.ds(CX0, CX), pl.ds(CY0, CY)] = coarse_forcing * cc[pl.ds(0, CX), pl.ds(0, CY)]
    rem_start()
    for x in (X0 - 1, X0 + PX):
        pc[:, x, mid] = pb[:, x, mid]

    theta = (UPPER + LOWER) / 2.0
    delta = (UPPER - LOWER) / 2.0
    ratio = delta / theta
    body_rows = pl.ds(CY0 - CW, CY + 2 * CW)
    cw_recv()
    p_start()
    rem_recv()
    rem_sent()

    def first_heading(x, _):
        heading = rem[x, body_rows] * (1.0 / theta)
        return [(ha, (x, body_rows), heading), (cor, (x, body_rows), heading)]

    planes(0, GX, first_heading, 6)

    def coarse_step(old, new, r0, n, keep, add):
        mid, above, below = pl.ds(r0, n), pl.ds(r0 + 1, n), pl.ds(r0 - 1, n)

        def body(x, _):
            v = old[x, mid]
            u = cw[2, x, mid]
            t = cw[0, x, mid] * old[x + 1, mid] + cw[0, x - 1, mid] * old[x - 1, mid]
            t = t + cw[1, x, mid] * old[x, above] + cw[1, x, below] * old[x, below]
            t = t + u * pltpu.roll(v, LANES - 1, 1) + pltpu.roll(u * v, 1, 1)
            left = rem[x, mid] - (v - t)
            heading = keep * v + add * left
            return [
                (rem, (x, mid), left),
                (new, (x, mid), heading),
                (cor, (x, mid), cor[x, mid] + heading),
            ]

        return body

    old, new = ha, hb
    for turn in range(1, CHEB):
        following = 1.0 / (2.0 * theta / delta - ratio)
        halo = CW - turn
        lo, hi = CX0 - halo, CX0 + CX + halo
        step = coarse_step(
            old, new, CY0 - halo, CY + 2 * halo, following * ratio, 2.0 * following / delta
        )
        planes(lo, hi, step, {16: 4, 14: 7, 12: 6, 10: 5, 8: 4}[hi - lo])
        ratio = following
        old, new = new, old

    inside = (pl.ds(CX0, CX), pl.ds(CY0, CY))
    near[inside] = cor[inside] * cc[pl.ds(0, CX), pl.ds(0, CY)]
    near_start()
    spread = lane_map(LANES, 2 * LANES, lambda i, o: o // 2 == i)

    def prolong(part, c, r, n, slot):
        x, r0 = X0 + 2 * (c - CX0), Y0 + 2 * (r - CY0)
        at = pl.ds(r0, 2 * n)
        stores = []
        for h in range(2):
            value = part[:, h * LANES : (h + 1) * LANES]
            ebuf[slot, h, pl.ds(r0, n, stride=2)] = value
            ebuf[slot, h, pl.ds(r0 + 1, n, stride=2)] = value
            for k in range(2):
                stores.append((pc, (h, x + k, at), pc[h, x + k, at] + ebuf[slot, h, at]))
        return stores

    zbuf[0, pl.ds(0, CX * CY)] = zdot(near[inside].reshape(CX * CY, LANES), spread)

    def prolong_inside(i, slot):
        part = zbuf[0, pl.ds(pl.multiple_of(i * CY, CY), CY)]
        return prolong(part, CX0 + i, CY0, CY, slot)

    planes(0, CX, prolong_inside, 4)
    edge = 12
    planes(X0 + 1, X0 + PX - 1, sweep(pc, pa, (R0 + edge, RN - 2 * edge)), 7)

    p_recv()
    near_recv()
    tall = CY + 8
    sides_x = (CX0 - 2, CX0 - 1, CX0 + CX, CX0 + CX + 1)
    for k, c in enumerate(sides_x):
        zbuf[1, pl.ds(k * tall, tall)] = zdot(near[c, pl.ds(CY0 - 2, tall)], spread)
    for k, r in enumerate((CY0 - 8, CY0 + CY)):
        strip = near[pl.ds(CX0, CX), pl.ds(r, 8)].reshape(CX * 8, LANES)
        zbuf[2, pl.ds(k * CX * 8, CX * 8)] = zdot(strip, spread)
    for k, c in enumerate(sides_x):
        part = zbuf[1, pl.ds(k * tall, CY + 4)]
        for ref, at, value in prolong(part, c, CY0 - 2, CY + 4, k):
            ref[at] = value

    for i in range(CX):
        low = zbuf[2, pl.ds(i * 8 + 6, 2)]
        high = zbuf[2, pl.ds(CX * 8 + i * 8, 2)]
        stores = prolong(low, CX0 + i, CY0 - 2, 2, i % 4)
        for ref, at, value in stores + prolong(high, CX0 + i, CY0 + CY, 2, i % 4):
            ref[at] = value
    for lo, hi in ((X0 - W + 1, X0 + 1), (X0 + PX - 1, X0 + PX + W - 1)):
        planes(lo, hi, sweep(pc, pa), 3)
    planes(X0 + 1, X0 + PX - 1, sweep(pc, pa, (R0, edge), (R0 + RN - edge, edge)), 7)
    p_sent()
    planes(X0 - 1, X0 + PX + 1, sweep(pa, pb), 6)

    ph_sent()
    src_sent()
    cw_sent()
    near_sent()


def finish(wx, wy, wz, dg, fo, pb, out_p, out_r, res, sem):
    copies = []
    for h in range(2):
        cols = pl.ds(h * LANES, LANES)
        block = pb.at[h, pl.ds(X0, PX), pl.ds(Y0, PY)]
        copies.append(pltpu.make_async_copy(block, out_p.at[:, :, cols], sem.at[h]))
        copies[-1].start()
    quarter = PX // 4
    for k in range(4):
        stores = []
        for x in range(k * quarter, (k + 1) * quarter):
            _, r = residual(pb, (wx, wy, wz), fo, dg, X0 + x)
            stores += [((x, pl.ds(0, PY), pl.ds(h * LANES, LANES)), r[h]) for h in range(2)]
        for at, value in stores:
            res[at] = value
        part = pl.ds(k * quarter, quarter)
        copies.append(pltpu.make_async_copy(res.at[part], out_r.at[part], sem.at[2 + k]))
        copies[-1].start()
    for copy in copies:
        copy.wait()


def per_device(source, phases):
    ns, ng = lax.axis_size("space"), lax.axis_size("group")
    fine = (2, FX, FY, LANES)
    coarse = (GX, GY, LANES)
    vmem = pltpu.VMEM
    scratch = [vmem(fine, jnp.int32)]
    scratch += [vmem(fine, F32)] * 5
    scratch += [vmem((3,) + coarse, F32), vmem((CX + 1, CS, LANES), F32)]
    scratch += [vmem(coarse, F32)] * 5
    scratch += [
        vmem((5, (CX + 1) * CS, 2 * LANES), F32),
        vmem((4, 2, PY, LANES), F32),
        vmem((4, 2, FY, LANES), F32),
        vmem((2, 1, LANES), F32),
        vmem((4 * ng, 1, LANES), F32),
        vmem((ns // 4, 1, LANES), F32),
        pltpu.SemaphoreType.DMA((2, 2)),
        pltpu.SemaphoreType.DMA((2,)),
        pltpu.SemaphoreType.DMA((2,)),
        pltpu.SemaphoreType.DMA((MESSAGES,)),
        pltpu.SemaphoreType.DMA((MESSAGES,)),
    ]
    fields = pl.pallas_call(
        functools.partial(kernel, ns, ng),
        out_shape=[jax.ShapeDtypeStruct(fine, F32)] * 6,
        in_specs=[pl.BlockSpec(memory_space=pltpu.HBM)] * 2,
        out_specs=[pl.BlockSpec(memory_space=pltpu.VMEM)] * 6,
        scratch_shapes=scratch,
        compiler_params=pltpu.CompilerParams(
            collective_id=0, has_side_effects=True, vmem_limit_bytes=40 * 2**20
        ),
    )(source, phases)
    return pl.pallas_call(
        finish,
        out_shape=[jax.ShapeDtypeStruct(source.shape, F32)] * 2,
        in_specs=[pl.BlockSpec(memory_space=pltpu.VMEM)] * 6,
        out_specs=[pl.BlockSpec(memory_space=pl.ANY)] * 2,
        scratch_shapes=[vmem(source.shape, F32), pltpu.SemaphoreType.DMA((6,))],
        compiler_params=pltpu.CompilerParams(vmem_limit_bytes=16 * 2**20),
    )(*fields)


def solution(mesh):
    spec = P("space", "group", None)
    return jax.shard_map(
        per_device, mesh=mesh, in_specs=(spec, spec), out_specs=(spec, spec), check_vma=False
    )
```
